512 devices in a mesh: ctx: 16 (over z), head: 8 (over y, x_hi), section: 4 (over x_lo, core).
Axes of the slice: x: 4 (x_hi: 2, x_lo: 2; x = x_hi * 2 + x_lo), y: 4, z: 16, core: 2. Of those that a mesh axis runs over, the one named last changes fastest.
Arguments:
- query_rows: bfloat16 [4, 4096, 3072], P('section', ('ctx', 'head')), may hold values from -6 to 6
- key_rows: bfloat16 [4, 4096, 1024], P('section', ('ctx', 'head')), may hold values from -6 to 6
- value_rows: bfloat16 [4, 4096, 1024], P('section', ('ctx', 'head')), may hold values from -6 to 6
- grad_out: bfloat16 [4, 4096, 3072], P('section', ('ctx', 'head')), may hold values from -6 to 6
- log_sum_exp: float32 [4, 24, 4096], P('section', None, ('ctx', 'head')), may hold values from 2 to 5
- delta_rows: float32 [4, 24, 4096], P('section', None, ('ctx', 'head')), may hold values from -16 to 16
- doc_lengths: int32 [4, 4], P('section'), may hold values from 1 to 2048, 4096 in all within a row
- block_map: int32 [16, 2], replicated, may hold values from 0 to 31, as said below
Outputs:
- grad_query: bfloat16 [4, 4096, 3072], P('section', ('ctx', 'head'))
- grad_key: bfloat16 [4, 4096, 1024], P('section', ('ctx', 'head'))
- grad_value: bfloat16 [4, 4096, 1024], P('section', ('ctx', 'head'))
The draws below stay inside these ranges and needn't reach their ends.
Inputs may be any that keep to these rules, and one draw needn't show every extreme that they name: Index i of ctx holds the sequence blocks block_map[i, 0] and block_map[i, 1] = 31 - block_map[i, 0]; column 0 holds each of 0 to 15 once. `doc_lengths`: each row sums to 4096; its longest document has exactly 2048 tokens.
All inputs are finite; a program needn't handle non-finite values.
Results may differ from the reference program's by a relative error of at most 0.013.
Values may be sent and summed in bfloat16 or wider, within the bound.
A program may use at most 64 MiB of HBM per device.

```python
import math
import jax
import jax.numpy as jnp
import numpy as np
from jax import lax

D_HEAD = 128
QH = 24
KVH = 8
BLOCK = 128
DOCS = 4
GROUP = 3
BLOCKS = 32
SEQ = 4096
DOC_MOST = 2048
SECTIONS = 4


def draw_block_map(key, part):
    key = jax.random.fold_in(key, 7)
    device_order = jax.random.permutation(key, BLOCKS // 2).astype(jnp.int32)
    return jnp.stack([device_order, BLOCKS - 1 - device_order], axis=1).astype(jnp.int32)


def level_of(stream_key, dims, split, low, high):
    factor_of, own = 1.0, jax.random.fold_in(stream_key, 6)
    for dim, parts in split:
        steps = jnp.exp(jax.random.uniform(jax.random.fold_in(own, dim), (parts,), jnp.float32, low / len(split), high / len(split)))
        factor_of = factor_of * jnp.repeat(steps, dims[dim] // parts).reshape([-1 if axis == dim else 1 for axis in range(len(dims))])
    return factor_of


def split_up(number_of, total, bound, slope):
    portions = [(1 << 20) // math.isqrt(standing ** slope) + 1 for standing in range(2, number_of + 1)]
    spare, holding = total - bound - (number_of - 1), [1] * (number_of - 1)
    while spare > 0:
        movable = [i for i in range(number_of - 1) if holding[i] < bound]
        whole, left = sum([portions[i] for i in movable]), spare
        for i in movable:
            addition = min(bound - holding[i], max(1, left * portions[i] // whole), spare)
            holding[i] = holding[i] + addition
            spare = spare - addition
    return np.array([bound] + holding)


def ragged(stream_key, count, total, limit, slope):
    if count == 2:
        one = jax.random.randint(stream_key, (), max(1, total - limit), min(limit, total - 1) + 1)
        return jnp.stack([one, total - one])
    sizes = jnp.asarray(split_up(count, total, limit, slope), jnp.int32)
    couples = (count - 1) // 2
    donor, receiver = sizes[1:1 + 2 * couples:2], sizes[2:2 + 2 * couples:2]
    room = jnp.minimum(donor - 1, limit - receiver)
    passed = jax.random.randint(jax.random.fold_in(stream_key, 1), (couples,), 0, 1 << 20) % (room + 1)
    sizes = sizes.at[1:1 + 2 * couples:2].set(donor - passed).at[2:2 + 2 * couples:2].set(receiver + passed)
    return sizes[jax.random.permutation(jax.random.fold_in(stream_key, 2), count)]


def scatter_about(stream_key, extent, scale, reach, split=(), held_as=jnp.bfloat16):
    array = scale * jax.random.normal(stream_key, extent, jnp.float32)
    if split:
        array = array * level_of(stream_key, extent, split, -0.22, 0.18)
    return jnp.clip(array, -reach, reach).astype(held_as)


def setup_inputs(seed: int = 0) -> dict:
    keys = jax.random.split(jax.random.key(seed), 9)
    return {
        "query_rows": scatter_about(keys[0], (SECTIONS, SEQ, QH * D_HEAD), 1.0, 6.0, ((0, 4), (1, 128))),
        "key_rows": scatter_about(keys[1], (SECTIONS, SEQ, KVH * D_HEAD), 1.0, 6.0, ((0, 4), (1, 128))),
        "value_rows": scatter_about(keys[2], (SECTIONS, SEQ, KVH * D_HEAD), 1.0, 6.0, ((0, 4), (1, 128))),
        "grad_out": scatter_about(keys[3], (SECTIONS, SEQ, QH * D_HEAD), 1.0, 6.0, ((0, 4), (1, 128))),
        "log_sum_exp": jnp.clip(2.0 + 3.0 * jax.random.uniform(keys[4], (SECTIONS, QH, SEQ), jnp.float32) ** level_of(keys[4], (SECTIONS, QH, SEQ), ((0, 4), (2, 128)), -0.2, 0.2), 2.0, 5.0),
        "delta_rows": scatter_about(keys[5], (SECTIONS, QH, SEQ), 4.0, 16.0, ((0, 4), (2, 128)), jnp.float32),
        "doc_lengths": jax.vmap(lambda own: ragged(own, DOCS, SEQ, DOC_MOST, 2))(jax.random.split(keys[6], SECTIONS)).reshape((SECTIONS, DOCS)).astype(jnp.int32),
        "block_map": draw_block_map(jax.random.fold_in(keys[8], 71), 0),
    }


def sequence_rows(block_map):
    block_ids = block_map.reshape(-1).astype(jnp.int32)
    holder = jnp.zeros((BLOCKS,), jnp.int32).at[block_ids].set(jnp.arange(BLOCKS, dtype=jnp.int32))
    seq_rows = holder[:, None] * BLOCK + jnp.arange(BLOCK, dtype=jnp.int32)[None, :]
    return seq_rows.reshape(SEQ).astype(jnp.int32)


def section_gradients(query_seq, key_seq, value_seq, grad_seq, lse_seq, delta_seq, lengths):
    score_scale = D_HEAD ** -0.5
    rows_block = SEQ // 8
    positions = jnp.arange(SEQ, dtype=jnp.int32)
    doc_ends = jnp.cumsum(lengths.astype(jnp.int32)).astype(jnp.int32)
    doc_ids = jnp.sum((doc_ends[None, :] <= positions[:, None]).astype(jnp.int32), axis=1).astype(jnp.int32)
    query_heads = query_seq.astype(jnp.float32).reshape(SEQ, KVH, GROUP, D_HEAD)
    grad_heads = grad_seq.astype(jnp.float32).reshape(SEQ, KVH, GROUP, D_HEAD)
    key_heads = key_seq.astype(jnp.float32).reshape(SEQ, KVH, D_HEAD)
    value_heads = value_seq.astype(jnp.float32).reshape(SEQ, KVH, D_HEAD)
    lse_heads = lse_seq.reshape(KVH, GROUP, SEQ)
    delta_heads = delta_seq.reshape(KVH, GROUP, SEQ)

    def one_block(totals, block_index):
        key_total, value_total = totals
        block_start = (block_index * rows_block).astype(jnp.int32)
        query_block = lax.dynamic_slice_in_dim(query_heads, block_start, rows_block, 0)
        grad_block = lax.dynamic_slice_in_dim(grad_heads, block_start, rows_block, 0)
        lse_block = lax.dynamic_slice_in_dim(lse_heads, block_start, rows_block, 2)
        delta_block = lax.dynamic_slice_in_dim(delta_heads, block_start, rows_block, 2)
        query_docs = lax.dynamic_slice_in_dim(doc_ids, block_start, rows_block, 0)
        query_pos = block_start + jnp.arange(rows_block, dtype=jnp.int32)
        allowed = (query_docs[:, None] == doc_ids[None, :]) & (positions[None, :] <= query_pos[:, None])
        scores = jnp.einsum('ikgd,jkd->kgij', query_block, key_heads) * score_scale
        weights = jnp.where(allowed, jnp.exp(scores - lse_block[..., None]), 0.0)
        weights_half = lax.optimization_barrier(weights.astype(jnp.bfloat16)).astype(jnp.float32)
        grad_prob = jnp.einsum('ikgd,jkd->kgij', grad_block, value_heads)
        dscore = weights * (grad_prob - delta_block[..., None])
        dscore = lax.optimization_barrier(dscore.astype(jnp.bfloat16)).astype(jnp.float32)
        value_part = jnp.einsum('kgij,ikgd->jkd', weights_half, grad_block)
        key_part = jnp.einsum('kgij,ikgd->jkd', dscore, query_block)
        query_part = jnp.einsum('kgij,jkd->ikgd', dscore, key_heads)
        return (key_total + key_part, value_total + value_part), query_part

    start_totals = (jnp.zeros((SEQ, KVH, D_HEAD), jnp.float32), jnp.zeros((SEQ, KVH, D_HEAD), jnp.float32))
    totals, query_parts = lax.scan(one_block, start_totals, jnp.arange(8, dtype=jnp.int32))
    query_grad = (query_parts.reshape(SEQ, QH * D_HEAD) * score_scale).astype(jnp.bfloat16)
    key_grad = (totals[0].reshape(SEQ, KVH * D_HEAD) * score_scale).astype(jnp.bfloat16)
    value_grad = totals[1].reshape(SEQ, KVH * D_HEAD).astype(jnp.bfloat16)
    return query_grad, key_grad, value_grad


def reference(query_rows, key_rows, value_rows, grad_out, log_sum_exp, delta_rows, doc_lengths, block_map):
    seq_rows = sequence_rows(block_map)
    query_list = []
    key_list = []
    value_list = []
    for section_index in range(SECTIONS):
        query_grad, key_grad, value_grad = section_gradients(
            query_rows[section_index][seq_rows], key_rows[section_index][seq_rows],
            value_rows[section_index][seq_rows], grad_out[section_index][seq_rows],
            log_sum_exp[section_index][:, seq_rows], delta_rows[section_index][:, seq_rows],
            doc_lengths[section_index])
        query_list.append(jnp.zeros_like(query_grad).at[seq_rows].set(query_grad))
        key_list.append(jnp.zeros_like(key_grad).at[seq_rows].set(key_grad))
        value_list.append(jnp.zeros_like(value_grad).at[seq_rows].set(value_grad))
    grad_query = jnp.roll(jnp.stack(query_list), -1, axis=0)
    grad_key = jnp.roll(jnp.stack(key_list), -1, axis=0)
    grad_value = jnp.roll(jnp.stack(value_list), -1, axis=0)
    return grad_query, grad_key, grad_value
```

```python
import functools

import jax
import jax.numpy as jnp
from jax import lax
from jax.experimental import pallas as pl
from jax.experimental.pallas import tpu as pltpu
from jax.sharding import PartitionSpec as P

D = 128
BLOCK = 128
GROUP = 3
LOG2E = 1.4426950408889634
MESH = pl.DeviceIdType.MESH


def kernel(
    sizes,
    lens,
    table,
    q_in,
    k_in,
    v_in,
    g_in,
    lse_in,
    delta_in,
    gq_out,
    gk_out,
    gv_out,
    q_own,
    g_own,
    q_stack,
    g_stack,
    q_turned,
    g_turned,
    kv,
    lse_raw,
    delta_raw,
    stat_out,
    stat_in,
    stat,
    dq,
    part,
    chain,
    oq,
    ok,
    ov,
    raw_sem,
    kv_sem,
    q_sem,
    g_sem,
    stat_sem,
    in_send,
    ag_send,
    ag_recv,
    rs_send,
    rs_recv,
    out_send,
    out_recv,
):
    n, heads, sections = sizes
    half = n // 2
    rows = q_in.shape[1]
    per_block = BLOCK // rows
    width = GROUP * D
    scale = D ** (-0.5)
    me = lax.axis_index("ctx")
    head = lax.axis_index("head")
    section = lax.axis_index("section")
    right, left = lax.rem(me + 1, n), lax.rem(me + n - 1, n)
    neighbour = (right, left)

    raw_lse = pltpu.make_async_copy(lse_in.at[0], lse_raw, raw_sem.at[0])
    raw_delta = pltpu.make_async_copy(delta_in.at[0], delta_raw, raw_sem.at[1])
    raw_lse.start()
    raw_delta.start()

    barrier = pltpu.get_barrier_semaphore()

    def greet(o, carry):
        pl.semaphore_signal(
            barrier, inc=1, device_id={"head": lax.rem(head + o, heads)}, device_id_type=MESH
        )
        return carry

    def greet_next(o, carry):
        pl.semaphore_signal(
            barrier,
            inc=1,
            device_id={
                "head": lax.rem(head + o, heads),
                "section": lax.rem(section + 1, sections),
            },
            device_id_type=MESH,
        )
        return carry

    lax.fori_loop(1, heads, greet, 0)
    for other in neighbour:
        pl.semaphore_signal(barrier, inc=1, device_id={"ctx": other}, device_id_type=MESH)
    lax.fori_loop(0, heads, greet_next, 0)
    pl.semaphore_wait(barrier, 2 * heads + 1)

    block_of, row_of = head // per_block, (head % per_block) * rows
    stat_half = rows * (head % per_block)

    def to_peer(src, dst, slot, sem, peer):
        return pltpu.make_async_remote_copy(
            src_ref=src,
            dst_ref=dst,
            send_sem=slot,
            recv_sem=sem,
            device_id={"head": peer},
            device_id_type=MESH,
        )

    def kv_slot(which):
        return kv.at[me, block_of, which, pl.ds(pl.multiple_of(row_of, rows), rows)]

    def kv_copies(o, peer):
        columns = pl.ds(pl.multiple_of(peer * D, D), D)
        return (
            to_peer(k_in.at[0, :, columns], kv_slot(0), in_send.at[0, o], kv_sem, peer),
            to_peer(v_in.at[0, :, columns], kv_slot(1), in_send.at[1, o], kv_sem, peer),
        )

    def wide_copies(o, peer):
        columns = pl.ds(pl.multiple_of(peer * width, width), width)
        own_rows = pl.ds(pl.multiple_of(head * rows, rows), rows)
        return (
            to_peer(q_in.at[0, :, columns], q_own.at[own_rows], in_send.at[2, o], q_sem, peer),
            to_peer(g_in.at[0, :, columns], g_own.at[own_rows], in_send.at[3, o], g_sem, peer),
        )

    def stat_copy(o, peer):
        return to_peer(stat_out.at[peer], stat_in.at[head], in_send.at[4, o], stat_sem, peer)

    def start_kv(o, carry):
        for copy in kv_copies(o, lax.rem(head + o, heads)):
            copy.start()
        return carry

    def start_wide(o, carry):
        for copy in wide_copies(o, lax.rem(head + o, heads)):
            copy.start()
        return carry

    def start_stat(o, carry):
        stat_copy(o, lax.rem(head + o, heads)).start()
        return carry

    def end_in(o, carry):
        peer = lax.rem(head + o, heads)
        for copy in kv_copies(o, peer) + wide_copies(o, peer) + (stat_copy(o, peer),):
            copy.wait_send()
        return carry

    lax.fori_loop(1, heads, start_kv, 0)
    own_narrow = pl.ds(pl.multiple_of(head * D, D), D)
    own_wide = pl.ds(pl.multiple_of(head * width, width), width)
    own_rows = pl.ds(pl.multiple_of(head * rows, rows), rows)
    pltpu.make_async_copy(k_in.at[0, :, own_narrow], kv_slot(0), kv_sem).start()
    pltpu.make_async_copy(v_in.at[0, :, own_narrow], kv_slot(1), kv_sem).start()
    lax.fori_loop(1, heads, start_wide, 0)
    pltpu.make_async_copy(q_in.at[0, :, own_wide], q_own.at[own_rows], q_sem).start()
    pltpu.make_async_copy(g_in.at[0, :, own_wide], g_own.at[own_rows], g_sem).start()

    raw_lse.wait()
    raw_delta.wait()
    lanes = lax.broadcasted_iota(jnp.int32, (1, BLOCK), 1)
    mine = (lanes >= stat_half) & (lanes < stat_half + rows)
    spread_lse = jnp.where(mine, jnp.concatenate([lse_raw[...]] * per_block, axis=1), 0.0)
    spread_delta = jnp.where(mine, jnp.concatenate([delta_raw[...]] * per_block, axis=1), 0.0)
    stat_out[...] = jnp.zeros_like(stat_out)
    for p in range(heads):
        stat_out[p, 0:GROUP] = spread_lse[p * GROUP : (p + 1) * GROUP] * LOG2E
        stat_out[p, GROUP : 2 * GROUP] = spread_delta[p * GROUP : (p + 1) * GROUP]
    lax.fori_loop(1, heads, start_stat, 0)
    pltpu.make_async_copy(stat_out.at[head], stat_in.at[head], stat_sem).start()

    def source(hops, d):
        return lax.rem(me + (n - hops if d == 0 else hops), n)

    def ag_copy(hop, d, c):
        slot = source(hop - 1, d)
        return pltpu.make_async_remote_copy(
            src_ref=kv.at[slot, c],
            dst_ref=kv.at[slot, c],
            send_sem=ag_send.at[d, c, hop],
            recv_sem=ag_recv.at[d, c, hop],
            device_id={"ctx": neighbour[d]},
            device_id_type=MESH,
        )

    def ag_arrived(hop, d, c):
        slot = source(hop, d)
        pltpu.make_async_copy(kv.at[slot, c], kv.at[slot, c], ag_recv.at[d, c, hop]).wait()

    pltpu.make_async_copy(kv.at[me], kv.at[me], kv_sem).wait()
    for c in range(2):
        for d in range(2):
            ag_copy(1, d, c).start()

    def lay_out():
        pltpu.make_async_copy(q_own, q_own, q_sem).wait()
        pltpu.make_async_copy(g_own, g_own, g_sem).wait()
        pltpu.make_async_copy(stat_in, stat_in, stat_sem).wait()
        for b in range(2):
            for h in range(GROUP):
                piece = slice((b * GROUP + h) * BLOCK, (b * GROUP + h + 1) * BLOCK)
                for own, stack, turned in (
                    (q_own, q_stack, q_turned),
                    (g_own, g_stack, g_turned),
                ):
                    tile = own[b * BLOCK : (b + 1) * BLOCK, h * D : (h + 1) * D]
                    stack[piece, :] = tile
                    turned[:, piece] = tile.T
            first = b * per_block
            total = stat_in[first]
            for p in range(1, per_block):
                total = total + stat_in[first + p]
            stat[b] = total
        dq[...] = jnp.zeros_like(dq)

    ends = [lens[0, 0]]
    for i in range(1, lens.shape[1]):
        ends.append(ends[-1] + lens[0, i])
    query_places, query_starts = [], []
    for b in range(2):
        places = table[me, b] * BLOCK + lanes
        starts = jnp.zeros_like(places)
        for end in ends:
            starts = jnp.where(places >= end, jnp.maximum(starts, end), starts)
        query_places.append(places)
        query_starts.append(starts)
    key_offsets = lax.broadcasted_iota(jnp.int32, (BLOCK, BLOCK), 0)

    def visit(j):
        for c in range(2):
            keys, values = kv[j, c, 0], kv[j, c, 1]
            pieces = slice(c * width, 2 * width)
            scores = jnp.dot(keys, q_turned[:, pieces], preferred_element_type=jnp.float32)
            grads = jnp.dot(values, g_turned[:, pieces], preferred_element_type=jnp.float32)
            key_places = table[j, c] * BLOCK + key_offsets
            weights, dscores = [], []
            for b in range(c, 2):
                live = (key_places <= query_places[b]) & (key_places >= query_starts[b])
                for h in range(GROUP):
                    at = ((b - c) * GROUP + h) * BLOCK
                    x = scores[:, at : at + BLOCK] * (scale * LOG2E) - stat[b, h : h + 1, :]
                    weight = jnp.where(live, jnp.exp2(x), 0.0)
                    dscore = weight * (
                        grads[:, at : at + BLOCK] - stat[b, GROUP + h : GROUP + h + 1, :]
                    )
                    weights.append(weight.astype(jnp.bfloat16))
                    dscores.append(dscore.astype(jnp.bfloat16))
            weight16 = jnp.concatenate(weights, axis=1)
            dscore16 = jnp.concatenate(dscores, axis=1)
            part[j, c, 0] = jnp.dot(
                dscore16, q_stack[pieces, :], preferred_element_type=jnp.float32
            )
            part[j, c, 1] = jnp.dot(
                weight16, g_stack[pieces, :], preferred_element_type=jnp.float32
            )
            dq[:, pieces] += jnp.dot(keys.T, dscore16, preferred_element_type=jnp.float32)

    def visit_number(i, carry):
        distance = (i + 1) // 2
        visit(lax.rem(me + n + distance * (2 * (i % 2) - 1), n))
        return carry

    per_turn = 3
    first_turn = half - (n - 1) // per_turn

    def forward(hop, last):
        for c in range(2):
            for d in range(2):
                ag_arrived(hop, d, c)
                if not last or c == d:
                    ag_copy(hop + 1, d, c).start()

    def turn(hop, carry):
        forward(hop, False)
        first = (hop - first_turn) * per_turn
        lax.fori_loop(first, first + per_turn, visit_number, 0)
        return carry

    def idle_turn(hop, carry):
        forward(hop, False)
        return carry

    lax.fori_loop(1, first_turn, idle_turn, 0)
    lay_out()
    lax.fori_loop(first_turn, half - 1, turn, 0)
    forward(half - 1, True)
    lax.fori_loop(n - 1 - per_turn, n - 1, visit_number, 0)

    def hops_of(d, c):
        return half if c == d else half - 1

    def rs_target(t, d, c):
        return source(n - (hops_of(d, c) + 1 - t), d)

    def rs_copy(t, d, c):
        return pltpu.make_async_remote_copy(
            src_ref=chain.at[d, c, t - 1],
            dst_ref=chain.at[d, c, t],
            send_sem=rs_send.at[d, c, t],
            recv_sem=rs_recv.at[d, c, t],
            device_id={"ctx": neighbour[d]},
            device_id_type=MESH,
        )

    def rs_arrived(t, d, c):
        pltpu.make_async_copy(chain.at[d, c, t], chain.at[d, c, t], rs_recv.at[d, c, t]).wait()

    def rs_begin(d, c):
        chain[d, c, 0] = part[rs_target(1, d, c), c].astype(jnp.bfloat16)
        rs_copy(1, d, c).start()

    def rs_pass(t, d, c):
        rs_arrived(t - 1, d, c)
        total = chain[d, c, t - 1].astype(jnp.float32) + part[rs_target(t, d, c), c]
        chain[d, c, t - 1] = total.astype(jnp.bfloat16)
        rs_copy(t, d, c).start()

    rs_begin(0, 1)
    rs_begin(1, 0)
    for c in range(2):
        ag_arrived(half, c, c)
    visit(lax.rem(me + half, n))
    rs_begin(0, 0)
    rs_begin(1, 1)

    down = lax.rem(section + sections - 1, sections)

    def out_copy(array, src, dst, columns, o):
        peer = lax.rem(head + o, heads)
        return pltpu.make_async_remote_copy(
            src_ref=src.at[pl.ds(pl.multiple_of(peer * rows, rows), rows)],
            dst_ref=dst.at[0, :, columns],
            send_sem=out_send.at[array, o],
            recv_sem=out_recv.at[array],
            device_id={"head": peer, "section": down},
            device_id_type=MESH,
        )

    for b in range(2):
        for h in range(GROUP):
            piece = slice((b * GROUP + h) * BLOCK, (b * GROUP + h + 1) * BLOCK)
            oq[b * BLOCK : (b + 1) * BLOCK, h * D : (h + 1) * D] = (
                (dq[:, piece] * scale).T.astype(jnp.bfloat16)
            )

    def start_query(o, carry):
        out_copy(0, oq, gq_out, own_wide, o).start()
        return carry

    lax.fori_loop(0, heads, start_query, 0)

    def rs_turn(t, carry):
        for d in range(2):
            rs_pass(t, d, 1 - d)
        for d in range(2):
            rs_pass(t, d, d)
        return carry

    lax.fori_loop(2, half, rs_turn, 0)
    for d in range(2):
        rs_pass(half, d, d)
    for d in range(2):
        rs_arrived(half - 1, d, 1 - d)
    for d in range(2):
        rs_arrived(half, d, d)
    for c in range(2):
        total = part[me, c]
        for d in range(2):
            total = total + chain[d, c, hops_of(d, c)].astype(jnp.float32)
        ok[c * BLOCK : (c + 1) * BLOCK, :] = (total[0] * scale).astype(jnp.bfloat16)
        ov[c * BLOCK : (c + 1) * BLOCK, :] = total[1].astype(jnp.bfloat16)

    def start_narrow(o, carry):
        out_copy(1, ok, gk_out, own_narrow, o).start()
        out_copy(2, ov, gv_out, own_narrow, o).start()
        return carry

    lax.fori_loop(0, heads, start_narrow, 0)

    lax.fori_loop(1, heads, end_in, 0)

    def end_ring(t, carry):
        for c in range(2):
            for d in range(2):
                ag_copy(t, d, c).wait_send()
                rs_copy(t, d, c).wait_send()
        return carry

    lax.fori_loop(1, half, end_ring, 0)
    for d in range(2):
        ag_copy(half, d, d).wait_send()
        rs_copy(half, d, d).wait_send()

    def end_out(o, carry):
        out_copy(0, oq, gq_out, own_wide, o).wait_send()
        out_copy(1, ok, gk_out, own_narrow, o).wait_send()
        out_copy(2, ov, gv_out, own_narrow, o).wait_send()
        return carry

    lax.fori_loop(0, heads, end_out, 0)
    for array, out in enumerate((gq_out, gk_out, gv_out)):
        pltpu.make_async_copy(out, out, out_recv.at[array]).wait()


def body(sizes, q, k, v, g, lse, delta, lens, table):
    n, heads, _ = sizes
    half = n // 2
    rows = q.shape[1]
    tokens = rows * heads
    bf16, f32 = jnp.bfloat16, jnp.float32
    any_space = pl.BlockSpec(memory_space=pl.ANY)
    smem = pl.BlockSpec(memory_space=pltpu.SMEM)
    dma = pltpu.SemaphoreType.DMA
    pieces = tokens * GROUP
    return pl.pallas_call(
        functools.partial(kernel, sizes),
        out_shape=(
            jax.ShapeDtypeStruct(q.shape, bf16),
            jax.ShapeDtypeStruct(k.shape, bf16),
            jax.ShapeDtypeStruct(v.shape, bf16),
        ),
        in_specs=[smem, smem] + [any_space] * 6,
        out_specs=(any_space,) * 3,
        scratch_shapes=[
            pltpu.VMEM((tokens, GROUP * D), bf16),
            pltpu.VMEM((tokens, GROUP * D), bf16),
            pltpu.VMEM((pieces, D), bf16),
            pltpu.VMEM((pieces, D), bf16),
            pltpu.VMEM((D, pieces), bf16),
            pltpu.VMEM((D, pieces), bf16),
            pltpu.VMEM((n, 2, 2, BLOCK, D), bf16),
            pltpu.VMEM((lse.shape[1], rows), f32),
            pltpu.VMEM((lse.shape[1], rows), f32),
            pltpu.VMEM((heads, 8, BLOCK), f32),
            pltpu.VMEM((heads, 8, BLOCK), f32),
            pltpu.VMEM((2, 8, BLOCK), f32),
            pltpu.VMEM((D, pieces), f32),
            pltpu.VMEM((n, 2, 2, BLOCK, D), f32),
            pltpu.VMEM((2, 2, half + 1, 2, BLOCK, D), bf16),
            pltpu.VMEM((tokens, GROUP * D), bf16),
            pltpu.VMEM((tokens, D), bf16),
            pltpu.VMEM((tokens, D), bf16),
            dma((2,)),
            dma,
            dma,
            dma,
            dma,
            dma((5, heads)),
            dma((2, 2, half + 1)),
            dma((2, 2, half + 1)),
            dma((2, 2, half + 1)),
            dma((2, 2, half + 1)),
            dma((3, heads)),
            dma((3,)),
        ],
        compiler_params=pltpu.CompilerParams(
            collective_id=0, has_side_effects=True, vmem_limit_bytes=40 * 1024 * 1024
        ),
    )(lens, table, q, k, v, g, lse, delta)


def solution(mesh):
    sizes = (mesh.shape["ctx"], mesh.shape["head"], mesh.shape["section"])
    tokens = P("section", ("ctx", "head"), None)
    totals = P("section", None, ("ctx", "head"))
    return jax.shard_map(
        functools.partial(body, sizes),
        mesh=mesh,
        in_specs=(tokens, tokens, tokens, tokens, totals, totals, P("section", None), P()),
        out_specs=(tokens, tokens, tokens),
        check_vma=False,
    )
```

```python
import functools

import jax
import jax.numpy as jnp
from jax import lax
from jax.experimental import pallas as pl
from jax.experimental.pallas import tpu as pltpu
from jax.sharding import PartitionSpec as P

D = 128
BLOCK = 128
GROUP = 3
RING = 4
PEERS = 8
RUN = 64
LOG2E = 1.4426950408889634
MESH = pl.DeviceIdType.MESH


def order_of(i):
    along_y = (0, 0, 0, 1, 1, 1, 3, 3, 3, 0, 1, 3, 2, 2, 2, 2)
    along_z = (0, 1, 3, 0, 1, 3, 0, 1, 3, 2, 2, 2, 2, 1, 3, 0)
    dy = sum(jnp.where(i == k, v, 0) for k, v in enumerate(along_y) if v)
    dr = sum(jnp.where(i == k, v, 0) for k, v in enumerate(along_z) if v)
    return dy, dr


def kernel(
    lens,
    table,
    q_in,
    k_in,
    v_in,
    g_in,
    lse_in,
    delta_in,
    gq_out,
    gk_out,
    gv_out,
    qg,
    q_stack,
    g_stack,
    q_turned,
    g_turned,
    kv,
    lse_raw,
    delta_raw,
    stat_out,
    stat_in,
    stat,
    dq,
    part,
    zs1,
    zr1,
    zs2,
    zr2,
    ys1,
    yr1,
    ys2,
    yr2,
    oq,
    okv,
    raw_sem,
    kv_sem,
    q_sem,
    stat_sem,
    in_send,
    ag1_send,
    ag1_recv,
    ag2_send,
    ag2_recv,
    yq1_send,
    yq1_recv,
    yq2_send,
    yq2_recv,
    yt_send,
    yt_recv,
    z1_send,
    z1_recv,
    z2_send,
    z2_recv,
    y1_send,
    y1_recv,
    y2_send,
    y2_recv,
    out_send,
    out_recv,
):
    rows = q_in.shape[1]
    width = GROUP * D
    scale = D ** (-0.5)
    sections = lax.axis_size("section")
    z, place, section = lax.axis_index("ctx"), lax.axis_index("head"), lax.axis_index("section")
    region, plane = z // RING, z % RING
    y, x = place // 2, place % 2
    mine = plane * 2 + x

    def peer_id(p):
        return {"ctx": region * RING + p // 2, "head": y * 2 + p % 2}

    def z_id(d):
        return {"ctx": lax.rem(z + (RING if d == 0 else 3 * RING), RING * RING)}

    def y_id(o):
        return {"head": lax.rem(y + o, RING) * 2 + x}

    y_step = (1, 3)

    def remote(src, dst, send, recv, where):
        return pltpu.make_async_remote_copy(
            src_ref=src,
            dst_ref=dst,
            send_sem=send,
            recv_sem=recv,
            device_id=where,
            device_id_type=MESH,
        )

    def landed(ref, sem):
        pltpu.make_async_copy(ref, ref, sem).wait()

    raw_lse = pltpu.make_async_copy(lse_in.at[0], lse_raw, raw_sem.at[0])
    raw_delta = pltpu.make_async_copy(delta_in.at[0], delta_raw, raw_sem.at[1])
    raw_lse.start()
    raw_delta.start()

    barrier = pltpu.get_barrier_semaphore()

    def greet(where):
        pl.semaphore_signal(barrier, inc=1, device_id=where, device_id_type=MESH)

    def greet_peer(o, carry):
        greet(peer_id(lax.rem(mine + o, PEERS)))
        return carry

    def greet_up(o, carry):
        greet({**peer_id(lax.rem(mine + o, PEERS)), "section": lax.rem(section + 1, sections)})
        return carry

    lax.fori_loop(1, PEERS, greet_peer, 0)
    for d in range(2):
        greet(z_id(d))
    for o in range(1, RING):
        greet(y_id(o))
    lax.fori_loop(0, PEERS, greet_up, 0)

    part[...] = jnp.zeros_like(part)
    dq[...] = jnp.zeros_like(dq)
    stat_out[...] = jnp.zeros_like(stat_out)
    raw_lse.wait()
    raw_delta.wait()
    lanes = lax.broadcasted_iota(jnp.int32, (1, BLOCK), 1)
    per_tile = BLOCK // rows
    first_lane = rows * (mine % per_tile)
    own_lanes = (lanes >= first_lane) & (lanes < first_lane + rows)
    spread_lse = jnp.where(own_lanes, jnp.concatenate([lse_raw[...]] * per_tile, axis=1), 0.0)
    spread_delta = jnp.where(own_lanes, jnp.concatenate([delta_raw[...]] * per_tile, axis=1), 0.0)
    for p in range(PEERS):
        stat_out[p, 0:GROUP] = spread_lse[p * GROUP : (p + 1) * GROUP] * LOG2E
        stat_out[p, GROUP : 2 * GROUP] = spread_delta[p * GROUP : (p + 1) * GROUP]
    pl.semaphore_wait(barrier, 2 * PEERS - 1 + 2 + RING - 1)

    own_rows = pl.ds(pl.multiple_of(mine * rows, rows), rows)

    def narrow(p):
        return pl.ds(pl.multiple_of(p * D, D), D)

    def wide(p):
        return pl.ds(pl.multiple_of(p * width, width), width)

    def kv_copies(p):
        return tuple(
            remote(src.at[0, :, narrow(p)], kv.at[region, i, own_rows], in_send.at[i, p], kv_sem, peer_id(p))
            for i, src in enumerate((k_in, v_in))
        )

    def q_copies(p):
        return tuple(
            remote(src.at[0, :, wide(p)], qg.at[y, mine, i], in_send.at[2 + i, p], q_sem.at[mine], peer_id(p))
            for i, src in enumerate((q_in, g_in))
        )

    def stat_copies(p):
        return (remote(stat_out.at[p], stat_in.at[mine], in_send.at[4, p], stat_sem, peer_id(p)),)

    def to_peers(copies):
        def one(o, carry):
            for copy in copies(lax.rem(mine + o, PEERS)):
                copy.start()
            return carry

        lax.fori_loop(1, PEERS, one, 0)

    to_peers(kv_copies)
    for i, src in enumerate((k_in, v_in)):
        pltpu.make_async_copy(src.at[0, :, narrow(mine)], kv.at[region, i, own_rows], kv_sem).start()
    to_peers(stat_copies)
    pltpu.make_async_copy(stat_out.at[mine], stat_in.at[mine], stat_sem).start()
    to_peers(q_copies)
    for i, src in enumerate((q_in, g_in)):
        pltpu.make_async_copy(src.at[0, :, wide(mine)], qg.at[y, mine, i], q_sem.at[mine]).start()

    def region_at(o):
        return lax.rem(region + o, RING)

    def ag1(d, i):
        return remote(
            kv.at[region, i], kv.at[region, i], ag1_send.at[d, i], ag1_recv.at[d, i], z_id(d)
        )

    def ag1_landed(d, i):
        landed(kv.at[region_at(3 if d == 0 else 1), i], ag1_recv.at[d, i])

    def ag2(d):
        held = kv.at[region_at(3 if d == 0 else 1), d]
        return remote(held, held, ag2_send.at[d], ag2_recv.at[d], z_id(d))

    landed(kv.at[region], kv_sem)
    for i in range(2):
        for d in range(2):
            ag1(d, (i + d) % 2).start()

    def y_at(o):
        return lax.rem(y + o, RING)

    def yq1(p, d):
        held = qg.at[y, p]
        return remote(held, held, yq1_send.at[d, p], yq1_recv.at[d, p], y_id(y_step[d]))

    def yq1_landed(p, d):
        landed(qg.at[y_at(3 if d == 0 else 1), p], yq1_recv.at[d, p])

    def yq2(p, d):
        held = qg.at[y_at(3 if d == 0 else 1), p]
        return remote(held, held, yq2_send.at[p], yq2_recv.at[p], y_id(y_step[d]))

    def yt(o):
        return remote(stat.at[y], stat.at[y], yt_send.at[o], yt_recv.at[o], y_id(o))

    landed(stat_in, stat_sem)
    for b in range(2):
        first = b * per_tile
        total = stat_in[first]
        for p in range(1, per_tile):
            total = total + stat_in[first + p]
        stat[y, b] = total
    for o in range(1, RING):
        yt(o).start()

    def pass_own(p, carry):
        landed(qg.at[y, p], q_sem.at[p])
        for d in range(2):
            yq1(p, d).start()
        return carry

    lax.fori_loop(0, PEERS, pass_own, 0)

    def lay_out(at):
        for b in range(2):
            for i, stack, turned in ((0, q_stack, q_turned), (1, g_stack, g_turned)):
                tile = qg[at, b * per_tile : (b + 1) * per_tile, i].reshape(BLOCK, width)
                for h in range(GROUP):
                    piece = slice((b * GROUP + h) * BLOCK, (b * GROUP + h + 1) * BLOCK)
                    own = tile[:, h * D : (h + 1) * D]
                    stack[at, piece, :] = own
                    turned[at, :, piece] = own.T

    ends = [lens[0, 0]]
    for i in range(1, lens.shape[1]):
        ends.append(ends[-1] + lens[0, i])
    run_lanes = lanes % RUN
    run_rows = lax.broadcasted_iota(jnp.int32, (RUN, BLOCK), 0)

    def visit(yq, r):
        key_start = (y % 2) * RUN
        key_places = jnp.concatenate(
            [table[r * RING + u, y // 2] * BLOCK + key_start + run_rows for u in range(RING)], axis=0
        )
        keys, values = kv[r, 0], kv[r, 1]
        turned_keys = keys.T
        for b in range(2):
            half = slice(b * width, (b + 1) * width)
            starts_at = [table[region * RING + 2 * b + u, yq // 2] * BLOCK for u in range(2)]
            places = jnp.where(lanes < RUN, starts_at[0], starts_at[1]) + (yq % 2) * RUN + run_lanes
            starts = jnp.zeros_like(places)
            for end in ends:
                starts = jnp.where(places >= end, jnp.maximum(starts, end), starts)
            live = (key_places <= places) & (key_places >= starts)
            scores = jnp.dot(keys, q_turned[yq, :, half], preferred_element_type=jnp.float32)
            grads = jnp.dot(values, g_turned[yq, :, half], preferred_element_type=jnp.float32)
            totals = stat[yq, b]
            weights, dscores = [], []
            for h in range(GROUP):
                at = slice(h * BLOCK, (h + 1) * BLOCK)
                exponent = scores[:, at] * (scale * LOG2E) - totals[h : h + 1, :]
                weight = jnp.where(live, jnp.exp2(exponent), 0.0)
                dscore = weight * (grads[:, at] - totals[GROUP + h : GROUP + h + 1, :])
                weights.append(weight.astype(jnp.bfloat16))
                dscores.append(dscore.astype(jnp.bfloat16))
            weight16 = jnp.concatenate(weights, axis=1)
            dscore16 = jnp.concatenate(dscores, axis=1)
            part[r, 0] += jnp.dot(dscore16, q_stack[yq, half, :], preferred_element_type=jnp.float32)
            part[r, 1] += jnp.dot(weight16, g_stack[yq, half, :], preferred_element_type=jnp.float32)
            dq[yq, b] += jnp.dot(turned_keys, dscore16, preferred_element_type=jnp.float32)

    def z1(d):
        return remote(zs1.at[d], zr1.at[d], z1_send.at[d], z1_recv.at[d], z_id(d))

    def z2(d, i):
        return remote(zs2.at[d, i], zr2.at[d, i], z2_send.at[d, i], z2_recv.at[d, i], z_id(d))

    def y1(d):
        return remote(ys1.at[d], yr1.at[d], y1_send.at[d], y1_recv.at[d], y_id(y_step[d]))

    def y2(d, b):
        return remote(ys2.at[d, b], yr2.at[d, b], y2_send.at[d, b], y2_recv.at[d, b], y_id(y_step[d]))

    def turn(i, carry):
        dy, dr = order_of(i)

        @pl.when(i == 1)
        def _():
            for d in range(2):
                ag1_landed(d, d)
                ag2(d).start()
            for p in range(PEERS):
                yq1_landed(p, p % 2)
                yq2(p, p % 2).start()
            for d in range(2):
                ag1_landed(d, 1 - d)

        @pl.when(i == 3)
        def _():
            for p in range(0, PEERS, 2):
                yq1_landed(p, 1)
            landed(stat.at[y_at(1)], yt_recv.at[3])

        @pl.when(i == 6)
        def _():
            for p in range(1, PEERS, 2):
                yq1_landed(p, 0)
            landed(stat.at[y_at(3)], yt_recv.at[1])

        @pl.when(i == 9)
        def _():
            for d in range(2):
                landed(kv.at[region_at(2), d], ag2_recv.at[d])

        @pl.when(i == 12)
        def _():
            for p in range(PEERS):
                landed(qg.at[y_at(2), p], yq2_recv.at[p])
            landed(stat.at[y_at(2)], yt_recv.at[2])

        yq, r = y_at(dy), region_at(dr)

        @pl.when((i == 0) | (i == 3) | (i == 6) | (i == 12))
        def _():
            lay_out(yq)

        @pl.when((y < 2) | (yq >= 2))
        def _():
            visit(yq, r)

        @pl.when(i == 12)
        def _():
            for d in range(2):
                zs1[d] = part[region_at(2), d].astype(jnp.bfloat16)
                z1(d).start()

        @pl.when(i == 14)
        def _():
            for d in range(2):
                zs2[d, 1 - d] = part[region_at(1 if d == 0 else 3), 1 - d].astype(jnp.bfloat16)
                z2(d, 1 - d).start()

        return carry

    lax.fori_loop(0, RING * RING, turn, 0)

    for d in range(2):
        ys1[d] = dq[y_at(2), d].astype(jnp.bfloat16)
        y1(d).start()
    for d in range(2):
        ys2[d, 1 - d] = dq[y_at(y_step[d]), 1 - d].astype(jnp.bfloat16)
        y2(d, 1 - d).start()
    for d in range(2):
        landed(zr1.at[d], z1_recv.at[d])
        total = part[region_at(1 if d == 0 else 3), d] + zr1[d].astype(jnp.float32)
        zs2[d, d] = total.astype(jnp.bfloat16)
        z2(d, d).start()
    for d in range(2):
        landed(yr1.at[d], y1_recv.at[d])
        total = dq[y_at(y_step[d]), d] + yr1[d].astype(jnp.float32)
        ys2[d, d] = total.astype(jnp.bfloat16)
        y2(d, d).start()

    down = lax.rem(section + sections - 1, sections)

    def out_copy(array, p):
        src, dst, columns = (
            (oq, gq_out, wide(mine)),
            (okv.at[0], gk_out, narrow(mine)),
            (okv.at[1], gv_out, narrow(mine)),
        )[array]
        return remote(
            src.at[pl.ds(pl.multiple_of(p * rows, rows), rows)],
            dst.at[0, :, columns],
            out_send.at[array, p],
            out_recv.at[array],
            {**peer_id(p), "section": down},
        )

    def hand_over(array):
        def one(o, carry):
            out_copy(array, lax.rem(mine + o, PEERS)).start()
            return carry

        lax.fori_loop(0, PEERS, one, 0)

    for b in range(2):
        total = dq[y, b]
        for d in range(2):
            landed(yr2.at[d, b], y2_recv.at[d, b])
            total = total + yr2[d, b].astype(jnp.float32)
        total = total * scale
        for h in range(GROUP):
            oq[b * BLOCK : (b + 1) * BLOCK, h * D : (h + 1) * D] = (
                total[:, h * BLOCK : (h + 1) * BLOCK].T.astype(jnp.bfloat16)
            )
    hand_over(0)
    for i in range(2):
        total = part[region, i]
        for d in range(2):
            landed(zr2.at[d, i], z2_recv.at[d, i])
            total = total + zr2[d, i].astype(jnp.float32)
        okv[i] = (total * scale if i == 0 else total).astype(jnp.bfloat16)
        hand_over(1 + i)

    def end_in(o, carry):
        p = lax.rem(mine + o, PEERS)
        for copy in kv_copies(p) + q_copies(p) + stat_copies(p):
            copy.wait_send()
        return carry

    lax.fori_loop(1, PEERS, end_in, 0)
    for d in range(2):
        for i in range(2):
            ag1(d, i).wait_send()
            z2(d, i).wait_send()
            y2(d, i).wait_send()
        ag2(d).wait_send()
        z1(d).wait_send()
        y1(d).wait_send()
    for o in range(1, RING):
        yt(o).wait_send()
    for p in range(PEERS):
        for d in range(2):
            yq1(p, d).wait_send()
        yq2(p, p % 2).wait_send()

    def end_out(p, carry):
        for array in range(3):
            out_copy(array, p).wait_send()
        return carry

    lax.fori_loop(0, PEERS, end_out, 0)
    for array, out in enumerate((gq_out, gk_out, gv_out)):
        landed(out, out_recv.at[array])


def body(q, k, v, g, lse, delta, lens, table):
    rows = q.shape[1]
    tokens = rows * PEERS
    width = GROUP * D
    pieces = tokens * GROUP
    bf16, f32 = jnp.bfloat16, jnp.float32
    any_space = pl.BlockSpec(memory_space=pl.ANY)
    smem = pl.BlockSpec(memory_space=pltpu.SMEM)
    dma = pltpu.SemaphoreType.DMA
    return pl.pallas_call(
        kernel,
        out_shape=(
            jax.ShapeDtypeStruct(q.shape, bf16),
            jax.ShapeDtypeStruct(k.shape, bf16),
            jax.ShapeDtypeStruct(v.shape, bf16),
        ),
        in_specs=[smem, smem] + [any_space] * 6,
        out_specs=(any_space,) * 3,
        scratch_shapes=[
            pltpu.VMEM((RING, PEERS, 2, rows, width), bf16),
            pltpu.VMEM((RING, pieces, D), bf16),
            pltpu.VMEM((RING, pieces, D), bf16),
            pltpu.VMEM((RING, D, pieces), bf16),
            pltpu.VMEM((RING, D, pieces), bf16),
            pltpu.VMEM((RING, 2, tokens, D), bf16),
            pltpu.VMEM((lse.shape[1], rows), f32),
            pltpu.VMEM((lse.shape[1], rows), f32),
            pltpu.VMEM((PEERS, 8, BLOCK), f32),
            pltpu.VMEM((PEERS, 8, BLOCK), f32),
            pltpu.VMEM((RING, 2, 8, BLOCK), f32),
            pltpu.VMEM((RING, 2, D, width), f32),
            pltpu.VMEM((RING, 2, tokens, D), f32),
            pltpu.VMEM((2, tokens, D), bf16),
            pltpu.VMEM((2, tokens, D), bf16),
            pltpu.VMEM((2, 2, tokens, D), bf16),
            pltpu.VMEM((2, 2, tokens, D), bf16),
            pltpu.VMEM((2, D, width), bf16),
            pltpu.VMEM((2, D, width), bf16),
            pltpu.VMEM((2, 2, D, width), bf16),
            pltpu.VMEM((2, 2, D, width), bf16),
            pltpu.VMEM((tokens, width), bf16),
            pltpu.VMEM((2, tokens, D), bf16),
            dma((2,)),
            dma,
            dma((PEERS,)),
            dma,
            dma((5, PEERS)),
            dma((2, 2)),
            dma((2, 2)),
            dma((2,)),
            dma((2,)),
            dma((2, PEERS)),
            dma((2, PEERS)),
            dma((PEERS,)),
            dma((PEERS,)),
            dma((RING,)),
            dma((RING,)),
            dma((2,)),
            dma((2,)),
            dma((2, 2)),
            dma((2, 2)),
            dma((2,)),
            dma((2,)),
            dma((2, 2)),
            dma((2, 2)),
            dma((3, PEERS)),
            dma((3,)),
        ],
        compiler_params=pltpu.CompilerParams(
            collective_id=0, has_side_effects=True, vmem_limit_bytes=60 * 1024 * 1024
        ),
    )(lens, table, q, k, v, g, lse, delta)


def solution(mesh):
    tokens = P("section", ("ctx", "head"), None)
    totals = P("section", None, ("ctx", "head"))
    return jax.shard_map(
        body,
        mesh=mesh,
        in_specs=(tokens, tokens, tokens, tokens, totals, totals, P("section", None), P()),
        out_specs=(tokens, tokens, tokens),
        check_vma=False,
    )
```

```python
import functools

import jax
import jax.numpy as jnp
from jax import lax
from jax.experimental import pallas as pl
from jax.experimental.pallas import tpu as pltpu
from jax.sharding import PartitionSpec as P

D = 128
BLOCK = 128
GROUP = 3
RING = 4
PEERS = 8
RUN = 64
LOG2E = 1.4426950408889634
AG_AT = (0, 1)
MESH = pl.DeviceIdType.MESH


def order_of(i):
    along_y = (0, 0, 0, 1, 1, 1, 3, 3, 3, 0, 1, 3, 2, 2, 2, 2)
    along_z = (0, 1, 3, 0, 1, 3, 0, 1, 3, 2, 2, 2, 2, 1, 3, 0)
    dy = sum(jnp.where(i == k, v, 0) for k, v in enumerate(along_y) if v)
    dr = sum(jnp.where(i == k, v, 0) for k, v in enumerate(along_z) if v)
    return dy, dr


def kernel(
    lens,
    table,
    q_in,
    k_in,
    v_in,
    g_in,
    lse_in,
    delta_in,
    gq_out,
    gk_out,
    gv_out,
    qg,
    q_stack,
    g_stack,
    q_turned,
    g_turned,
    kv,
    lse_raw,
    delta_raw,
    stat_out,
    stat_in,
    stat,
    dq,
    part,
    zs1,
    zr1,
    zs2,
    zr2,
    ys1,
    yr1,
    ys2,
    yr2,
    oq,
    okv,
    lens_held,
    table_held,
    raw_sem,
    kv_sem,
    q_sem,
    stat_sem,
    in_send,
    ag1_send,
    ag1_recv,
    ag2_send,
    ag2_recv,
    yq1_send,
    yq1_recv,
    yq2_send,
    yq2_recv,
    yt_send,
    yt_recv,
    z1_send,
    z1_recv,
    z2_send,
    z2_recv,
    y1_send,
    y1_recv,
    y2_send,
    y2_recv,
    out_send,
    out_recv,
):
    rows = q_in.shape[1]
    width = GROUP * D
    scale = D ** (-0.5)
    sections = lax.axis_size("section")
    z, place, section = lax.axis_index("ctx"), lax.axis_index("head"), lax.axis_index("section")
    planes = RING * RING
    region, plane = z // RING, z % RING
    y, x = place // 2, place % 2
    mine = plane * 2 + x

    def piece_plane(at, along_y, u):
        return lax.rem(at + planes - 2 + along_y % 2 + u, planes)

    def from_id(p):
        return {"ctx": piece_plane(z, y, p // 2), "head": y * 2 + p % 2}

    def to_plane(k):
        return lax.rem(z + planes + 2 - y % 2 - k, planes)

    def to_id(k):
        return {"ctx": to_plane(k // 2), "head": y * 2 + k % 2}

    def head_of(k):
        return (to_plane(k // 2) % RING) * 2 + k % 2

    def piece_of(k):
        return (k // 2) * 2 + x

    self_at = (2 - y % 2) * 2 + x

    def z_id(d):
        return {"ctx": lax.rem(z + (RING if d == 0 else 3 * RING), RING * RING)}

    def y_id(o):
        return {"head": lax.rem(y + o, RING) * 2 + x}

    y_step = (1, 3)

    def remote(src, dst, send, recv, where):
        return pltpu.make_async_remote_copy(
            src_ref=src,
            dst_ref=dst,
            send_sem=send,
            recv_sem=recv,
            device_id=where,
            device_id_type=MESH,
        )

    def landed(ref, sem):
        pltpu.make_async_copy(ref, ref, sem).wait()

    raw_lse = pltpu.make_async_copy(lse_in.at[0], lse_raw, raw_sem.at[0])
    raw_delta = pltpu.make_async_copy(delta_in.at[0], delta_raw, raw_sem.at[1])
    raw_lens = pltpu.make_async_copy(lens, lens_held, raw_sem.at[2])
    raw_table = pltpu.make_async_copy(table, table_held, raw_sem.at[3])
    for copy in (raw_lse, raw_delta, raw_lens, raw_table):
        copy.start()

    barrier = pltpu.get_barrier_semaphore()

    def greet(where):
        pl.semaphore_signal(barrier, inc=1, device_id=where, device_id_type=MESH)

    def greet_peer(o, carry):
        greet(from_id(lax.rem(self_at + o, PEERS)))
        return carry

    def greet_up(o, carry):
        greet({**to_id(lax.rem(self_at + o, PEERS)), "section": lax.rem(section + 1, sections)})
        return carry

    lax.fori_loop(1, PEERS, greet_peer, 0)
    for d in range(2):
        greet(z_id(d))
    for o in range(1, RING):
        greet(y_id(o))
    lax.fori_loop(0, PEERS, greet_up, 0)

    part[...] = jnp.zeros_like(part)
    dq[...] = jnp.zeros_like(dq)
    stat_out[...] = jnp.zeros_like(stat_out)
    for copy in (raw_lse, raw_delta, raw_lens, raw_table):
        copy.wait()
    lanes = lax.broadcasted_iota(jnp.int32, (1, BLOCK), 1)
    per_tile = BLOCK // rows
    wide_lse = jnp.concatenate([lse_raw[...]] * per_tile, axis=1) * LOG2E
    wide_delta = jnp.concatenate([delta_raw[...]] * per_tile, axis=1)
    for p in range(PEERS):
        k = lax.rem(z + 2 - y % 2 - p // 2 + planes, RING)
        first_lane = rows * ((k % 2) * 2 + x)
        own_lanes = (lanes >= first_lane) & (lanes < first_lane + rows)
        of_head = slice(p * GROUP, (p + 1) * GROUP)
        stat_out[p, 0:GROUP] = jnp.where(own_lanes, wide_lse[of_head], 0.0)
        stat_out[p, GROUP : 2 * GROUP] = jnp.where(own_lanes, wide_delta[of_head], 0.0)
    pl.semaphore_wait(barrier, 2 * PEERS - 1 + 2 + RING - 1)

    def narrow(h):
        return pl.ds(pl.multiple_of(h * D, D), D)

    def wide(h):
        return pl.ds(pl.multiple_of(h * width, width), width)

    def rows_of(p):
        return pl.ds(pl.multiple_of(p * rows, rows), rows)

    def kv_copies(k):
        return tuple(
            remote(
                src.at[0, :, narrow(head_of(k))],
                kv.at[region_of(k), i, rows_of(piece_of(k))],
                in_send.at[i, k],
                kv_sem,
                to_id(k),
            )
            for i, src in enumerate((k_in, v_in))
        )

    def region_of(k):
        return to_plane(k // 2) // RING

    def q_copies(k):
        return tuple(
            remote(
                src.at[0, :, wide(head_of(k))],
                qg.at[y, piece_of(k), i],
                in_send.at[2 + i, k],
                q_sem.at[piece_of(k)],
                to_id(k),
            )
            for i, src in enumerate((q_in, g_in))
        )

    def stat_copies(k):
        return (
            remote(
                stat_out.at[head_of(k)],
                stat_in.at[piece_of(k)],
                in_send.at[4, k],
                stat_sem,
                to_id(k),
            ),
        )

    def to_peers(copies):
        def one(o, carry):
            for copy in copies(lax.rem(self_at + o, PEERS)):
                copy.start()
            return carry

        lax.fori_loop(1, PEERS, one, 0)

    to_peers(kv_copies)
    for i, src in enumerate((k_in, v_in)):
        pltpu.make_async_copy(src.at[0, :, narrow(mine)], kv.at[region, i, rows_of(self_at)], kv_sem).start()
    to_peers(stat_copies)
    pltpu.make_async_copy(stat_out.at[mine], stat_in.at[self_at], stat_sem).start()
    to_peers(q_copies)
    for i, src in enumerate((q_in, g_in)):
        pltpu.make_async_copy(src.at[0, :, wide(mine)], qg.at[y, self_at, i], q_sem.at[self_at]).start()

    def region_at(o):
        return lax.rem(region + o, RING)

    def tile_of(c):
        return pl.ds(c * BLOCK, BLOCK)

    def ag1(d, i, c):
        held = kv.at[region, i, tile_of(c)]
        return remote(held, held, ag1_send.at[d, i, c], ag1_recv.at[d, i, c], z_id(d))

    def ag1_landed(d, i, c):
        landed(kv.at[region_at(3 if d == 0 else 1), i, tile_of(c)], ag1_recv.at[d, i, c])

    def ag2(d, c):
        held = kv.at[region_at(3 if d == 0 else 1), d, tile_of(c)]
        return remote(held, held, ag2_send.at[d, c], ag2_recv.at[d, c], z_id(d))

    def y_at(o):
        return lax.rem(y + o, RING)

    def yq1(p, d):
        held = qg.at[y, p]
        return remote(held, held, yq1_send.at[d, p], yq1_recv.at[d, p], y_id(y_step[d]))

    def yq1_landed(p, d):
        landed(qg.at[y_at(3 if d == 0 else 1), p], yq1_recv.at[d, p])

    def yq2(p, d):
        held = qg.at[y_at(3 if d == 0 else 1), p]
        return remote(held, held, yq2_send.at[p], yq2_recv.at[p], y_id(y_step[d]))

    def yt(o):
        return remote(stat.at[y], stat.at[y], yt_send.at[o], yt_recv.at[o], y_id(o))

    def pass_own(p):
        landed(qg.at[y, p], q_sem.at[p])
        for d in range(2):
            yq1(p, d).start()

    def nearest(odd, j):
        even_first = (2, 1, 3, 0)[j]
        return even_first + odd * ((1, 0, 2, 3)[j] - even_first)

    pass_own(self_at)
    landed(kv.at[region], kv_sem)
    for i in range(2):
        for c in range(2):
            for d in range(2):
                ag1(d, (i + d) % 2, c).start()
    for j in range(RING):
        u = nearest(y % 2, j)
        if j == 0:
            pass_own(2 * u + 1 - x)
        else:
            pass_own(2 * u)
            pass_own(2 * u + 1)

    landed(stat_in, stat_sem)
    for b in range(2):
        first = b * per_tile
        total = stat_in[first]
        for p in range(1, per_tile):
            total = total + stat_in[first + p]
        stat[y, b] = total
    for o in range(1, RING):
        yt(o).start()


    def lay_out(at):
        for b in range(2):
            for i, stack, turned in ((0, q_stack, q_turned), (1, g_stack, g_turned)):
                tile = qg[at, b * per_tile : (b + 1) * per_tile, i].reshape(BLOCK, width)
                for h in range(GROUP):
                    piece = slice((b * GROUP + h) * BLOCK, (b * GROUP + h + 1) * BLOCK)
                    own = tile[:, h * D : (h + 1) * D]
                    stack[at, piece, :] = own
                    turned[at, :, piece] = own.T

    ends = [lens_held[0, 0]]
    for i in range(1, lens.shape[1]):
        ends.append(ends[-1] + lens_held[0, i])
    run_lanes = lanes % RUN
    run_rows = lax.broadcasted_iota(jnp.int32, (RUN, BLOCK), 0)

    def visit(yq, r):
        key_start = (y % 2) * RUN
        key_places = jnp.concatenate(
            [
                table_held[y // 2, piece_plane(r * RING + plane, y, u)] * BLOCK + key_start + run_rows
                for u in range(RING)
            ],
            axis=0,
        )
        keys, values = kv[r, 0], kv[r, 1]
        turned_keys = keys.T
        for b in range(2):
            half = slice(b * width, (b + 1) * width)
            starts_at = [table_held[yq // 2, piece_plane(z, yq, 2 * b + u)] * BLOCK for u in range(2)]
            places = jnp.where(lanes < RUN, starts_at[0], starts_at[1]) + (yq % 2) * RUN + run_lanes
            starts = jnp.zeros_like(places)
            for end in ends:
                starts = jnp.where(places >= end, jnp.maximum(starts, end), starts)
            live = (key_places <= places) & (key_places >= starts)
            scores = jnp.dot(keys, q_turned[yq, :, half], preferred_element_type=jnp.float32)
            grads = jnp.dot(values, g_turned[yq, :, half], preferred_element_type=jnp.float32)
            totals = stat[yq, b]
            weights, dscores = [], []
            for h in range(GROUP):
                at = slice(h * BLOCK, (h + 1) * BLOCK)
                exponent = scores[:, at] * (scale * LOG2E) - totals[h : h + 1, :]
                weight = jnp.where(live, jnp.exp2(exponent), 0.0)
                dscore = weight * (grads[:, at] - totals[GROUP + h : GROUP + h + 1, :])
                weights.append(weight.astype(jnp.bfloat16))
                dscores.append(dscore.astype(jnp.bfloat16))
            weight16 = jnp.concatenate(weights, axis=1)
            dscore16 = jnp.concatenate(dscores, axis=1)
            part[r, 0] += jnp.dot(dscore16, q_stack[yq, half, :], preferred_element_type=jnp.float32)
            part[r, 1] += jnp.dot(weight16, g_stack[yq, half, :], preferred_element_type=jnp.float32)
            dq[yq, b] += jnp.dot(turned_keys, dscore16, preferred_element_type=jnp.float32)

    def z1(d, c):
        return remote(
            zs1.at[d, tile_of(c)], zr1.at[d, tile_of(c)], z1_send.at[d, c], z1_recv.at[d, c], z_id(d)
        )

    def z2(d, i, c):
        return remote(
            zs2.at[d, i, tile_of(c)],
            zr2.at[d, i, tile_of(c)],
            z2_send.at[d, i, c],
            z2_recv.at[d, i, c],
            z_id(d),
        )

    def y1(d):
        return remote(ys1.at[d], yr1.at[d], y1_send.at[d], y1_recv.at[d], y_id(y_step[d]))

    def y2(d, b):
        return remote(ys2.at[d, b], yr2.at[d, b], y2_send.at[d, b], y2_recv.at[d, b], y_id(y_step[d]))

    def turn(i, carry):
        dy, dr = order_of(i)

        @pl.when(i == 1)
        def _():
            for j in range(RING):
                for d in range(2):
                    p = 2 * nearest(1 - y % 2, j) + d
                    yq1_landed(p, d)
                    yq2(p, d).start()
                if j in AG_AT:
                    c = AG_AT.index(j)
                    for d in range(2):
                        ag1_landed(d, d, c)
                        ag2(d, c).start()
            for c in range(2):
                for d in range(2):
                    ag1_landed(d, 1 - d, c)

        @pl.when(i == 3)
        def _():
            for p in range(0, PEERS, 2):
                yq1_landed(p, 1)
            landed(stat.at[y_at(1)], yt_recv.at[3])

        @pl.when(i == 6)
        def _():
            for p in range(1, PEERS, 2):
                yq1_landed(p, 0)
            landed(stat.at[y_at(3)], yt_recv.at[1])

        @pl.when(i == 9)
        def _():
            for c in range(2):
                for d in range(2):
                    landed(kv.at[region_at(2), d, tile_of(c)], ag2_recv.at[d, c])

        @pl.when(i == 12)
        def _():
            for p in range(PEERS):
                landed(qg.at[y_at(2), p], yq2_recv.at[p])
            landed(stat.at[y_at(2)], yt_recv.at[2])

        @pl.when(i == 13)
        def _():
            for d in range(2):
                zs1[d] = part[region_at(2), d].astype(jnp.bfloat16)
            for c in range(2):
                for d in range(2):
                    z1(d, c).start()

        @pl.when(i == 15)
        def _():
            for d in range(2):
                side = region_at(1 if d == 0 else 3)
                zs2[d, 1 - d] = part[side, 1 - d].astype(jnp.bfloat16)
                for c in range(2):
                    z2(d, 1 - d, c).start()

        yq, r = y_at(dy), region_at(dr)

        @pl.when((i == 0) | (i == 3) | (i == 6) | (i == 12))
        def _():
            lay_out(yq)

        @pl.when((y < 2) | (yq >= 2))
        def _():
            visit(yq, r)

        return carry

    lax.fori_loop(0, RING * RING, turn, 0)

    for d in range(2):
        ys1[d] = dq[y_at(2), d].astype(jnp.bfloat16)
        y1(d).start()
    for d in range(2):
        ys2[d, 1 - d] = dq[y_at(y_step[d]), 1 - d].astype(jnp.bfloat16)
        y2(d, 1 - d).start()
    for d in range(2):
        landed(yr1.at[d], y1_recv.at[d])
        total = dq[y_at(y_step[d]), d] + yr1[d].astype(jnp.float32)
        ys2[d, d] = total.astype(jnp.bfloat16)
        y2(d, d).start()
    for c in range(2):
        for d in range(2):
            landed(zr1.at[d, tile_of(c)], z1_recv.at[d, c])
            side = region_at(1 if d == 0 else 3)
            total = part[side, d, tile_of(c)] + zr1[d, tile_of(c)].astype(jnp.float32)
            zs2[d, d, tile_of(c)] = total.astype(jnp.bfloat16)
            z2(d, d, c).start()

    down = lax.rem(section + sections - 1, sections)

    def out_copy(array, p):
        src, dst, columns = (
            (oq, gq_out, wide(mine)),
            (okv.at[0], gk_out, narrow(mine)),
            (okv.at[1], gv_out, narrow(mine)),
        )[array]
        return remote(
            src.at[rows_of(p)],
            dst.at[0, :, columns],
            out_send.at[array, p],
            out_recv.at[array],
            {**from_id(p), "section": down},
        )

    def hand_over(array):
        def one(o, carry):
            out_copy(array, lax.rem(self_at + o, PEERS)).start()
            return carry

        lax.fori_loop(0, PEERS, one, 0)

    for b in range(2):
        total = dq[y, b]
        for d in range(2):
            landed(yr2.at[d, b], y2_recv.at[d, b])
            total = total + yr2[d, b].astype(jnp.float32)
        total = total * scale
        for h in range(GROUP):
            oq[b * BLOCK : (b + 1) * BLOCK, h * D : (h + 1) * D] = (
                total[:, h * BLOCK : (h + 1) * BLOCK].T.astype(jnp.bfloat16)
            )
    hand_over(0)
    for i in range(2):
        total = part[region, i]
        for d in range(2):
            for c in range(2):
                landed(zr2.at[d, i, tile_of(c)], z2_recv.at[d, i, c])
            total = total + zr2[d, i].astype(jnp.float32)
        okv[i] = (total * scale if i == 0 else total).astype(jnp.bfloat16)
        hand_over(1 + i)

    def end_in(o, carry):
        k = lax.rem(self_at + o, PEERS)
        for copy in kv_copies(k) + q_copies(k) + stat_copies(k):
            copy.wait_send()
        return carry

    lax.fori_loop(1, PEERS, end_in, 0)
    for d in range(2):
        for i in range(2):
            for c in range(2):
                ag1(d, i, c).wait_send()
                z2(d, i, c).wait_send()
            y2(d, i).wait_send()
        for c in range(2):
            ag2(d, c).wait_send()
            z1(d, c).wait_send()
        y1(d).wait_send()
    for o in range(1, RING):
        yt(o).wait_send()
    for p in range(PEERS):
        for d in range(2):
            yq1(p, d).wait_send()
        yq2(p, p % 2).wait_send()

    def end_out(p, carry):
        for array in range(3):
            out_copy(array, p).wait_send()
        return carry

    lax.fori_loop(0, PEERS, end_out, 0)
    for array, out in enumerate((gq_out, gk_out, gv_out)):
        landed(out, out_recv.at[array])


def settle(*refs):
    loads = [pltpu.make_async_copy(refs[i], refs[6 + i], refs[9].at[0, i]) for i in range(3)]
    stores = [pltpu.make_async_copy(refs[6 + i], refs[3 + i], refs[9].at[1, i]) for i in range(3)]
    for copy in loads:
        copy.start()
    for load, store in zip(loads, stores):
        load.wait()
        store.start()
    for copy in stores:
        copy.wait()


def body(q, k, v, g, lse, delta, lens, table):
    rows = q.shape[1]
    tokens = rows * PEERS
    width = GROUP * D
    pieces = tokens * GROUP
    bf16, f32 = jnp.bfloat16, jnp.float32
    any_space = pl.BlockSpec(memory_space=pl.ANY)
    dma = pltpu.SemaphoreType.DMA
    handed = pl.pallas_call(
        kernel,
        out_shape=(
            jax.ShapeDtypeStruct(q.shape, bf16),
            jax.ShapeDtypeStruct(k.shape, bf16),
            jax.ShapeDtypeStruct(v.shape, bf16),
        ),
        in_specs=[any_space] * 8,
        out_specs=(any_space,) * 3,
        scratch_shapes=[
            pltpu.VMEM((RING, PEERS, 2, rows, width), bf16),
            pltpu.VMEM((RING, pieces, D), bf16),
            pltpu.VMEM((RING, pieces, D), bf16),
            pltpu.VMEM((RING, D, pieces), bf16),
            pltpu.VMEM((RING, D, pieces), bf16),
            pltpu.VMEM((RING, 2, tokens, D), bf16),
            pltpu.VMEM((lse.shape[1], rows), f32),
            pltpu.VMEM((lse.shape[1], rows), f32),
            pltpu.VMEM((PEERS, 8, BLOCK), f32),
            pltpu.VMEM((PEERS, 8, BLOCK), f32),
            pltpu.VMEM((RING, 2, 8, BLOCK), f32),
            pltpu.VMEM((RING, 2, D, width), f32),
            pltpu.VMEM((RING, 2, tokens, D), f32),
            pltpu.VMEM((2, tokens, D), bf16),
            pltpu.VMEM((2, tokens, D), bf16),
            pltpu.VMEM((2, 2, tokens, D), bf16),
            pltpu.VMEM((2, 2, tokens, D), bf16),
            pltpu.VMEM((2, D, width), bf16),
            pltpu.VMEM((2, D, width), bf16),
            pltpu.VMEM((2, 2, D, width), bf16),
            pltpu.VMEM((2, 2, D, width), bf16),
            pltpu.VMEM((tokens, width), bf16),
            pltpu.VMEM((2, tokens, D), bf16),
            pltpu.SMEM(lens.shape, jnp.int32),
            pltpu.SMEM(table.shape[::-1], jnp.int32),
            dma((4,)),
            dma,
            dma((PEERS,)),
            dma,
            dma((5, PEERS)),
            dma((2, 2, 2)),
            dma((2, 2, 2)),
            dma((2, 2)),
            dma((2, 2)),
            dma((2, PEERS)),
            dma((2, PEERS)),
            dma((PEERS,)),
            dma((PEERS,)),
            dma((RING,)),
            dma((RING,)),
            dma((2, 2)),
            dma((2, 2)),
            dma((2, 2, 2)),
            dma((2, 2, 2)),
            dma((2,)),
            dma((2,)),
            dma((2, 2)),
            dma((2, 2)),
            dma((3, PEERS)),
            dma((3,)),
        ],
        compiler_params=pltpu.CompilerParams(
            collective_id=0, has_side_effects=True, vmem_limit_bytes=60 * 1024 * 1024
        ),
    )(lens, table.T, q, k, v, g, lse, delta)
    return pl.pallas_call(
        settle,
        out_shape=tuple(jax.ShapeDtypeStruct(out.shape, out.dtype) for out in handed),
        in_specs=[any_space] * 3,
        out_specs=(any_space,) * 3,
        scratch_shapes=[pltpu.VMEM(out.shape, out.dtype) for out in handed] + [dma((2, 3))],
        compiler_params=pltpu.CompilerParams(vmem_limit_bytes=60 * 1024 * 1024),
    )(*handed)


def solution(mesh):
    tokens = P("section", ("ctx", "head"), None)
    totals = P("section", None, ("ctx", "head"))
    return jax.shard_map(
        body,
        mesh=mesh,
        in_specs=(tokens, tokens, tokens, tokens, totals, totals, P("section", None), P()),
        out_specs=(tokens, tokens, tokens),
        check_vma=False,
    )
```

```python
import functools

import jax
import jax.numpy as jnp
from jax import lax
from jax.experimental import pallas as pl
from jax.experimental.pallas import tpu as pltpu
from jax.sharding import PartitionSpec as P

D = 128
BLOCK = 128
GROUP = 3
RING = 4
PEERS = 8
RUN = 64
LOG2E = 1.4426950408889634
AG_AT = (0, 1)
MESH = pl.DeviceIdType.MESH


def pick(i, values):
    return sum(jnp.where(i == k, v, 0) for k, v in enumerate(values) if v)


def kernel(
    lens,
    table,
    q_in,
    k_in,
    v_in,
    g_in,
    lse_in,
    delta_in,
    gq_out,
    gk_out,
    gv_out,
    qg,
    q_stack,
    g_stack,
    q_turned,
    g_turned,
    kv,
    lse_raw,
    delta_raw,
    stat_out,
    stat_in,
    stat,
    dq,
    part,
    zs1,
    zr1,
    zs2,
    zr2,
    ys1,
    yr1,
    ys2,
    yr2,
    oq,
    okv,
    lens_held,
    table_held,
    raw_sem,
    kv_sem,
    q_sem,
    stat_sem,
    in_send,
    ag1_send,
    ag1_recv,
    ag2_send,
    ag2_recv,
    yq1_send,
    yq1_recv,
    yq2_send,
    yq2_recv,
    yt_send,
    yt_recv,
    z1_send,
    z1_recv,
    z2_send,
    z2_recv,
    y1_send,
    y1_recv,
    y2_send,
    y2_recv,
    out_send,
    out_recv,
):
    rows = q_in.shape[1]
    width = GROUP * D
    scale = D ** (-0.5)
    sections = lax.axis_size("section")
    z, place, section = lax.axis_index("ctx"), lax.axis_index("head"), lax.axis_index("section")
    planes = RING * RING
    region, plane = z // RING, z % RING
    y, x = place // 2, place % 2
    mine = plane * 2 + x

    def piece_plane(at, along_y, u):
        return lax.rem(at + planes - 2 + along_y % 2 + u, planes)

    def from_id(p):
        return {"ctx": piece_plane(z, y, p // 2), "head": y * 2 + p % 2}

    def to_plane(k):
        return lax.rem(z + planes + 2 - y % 2 - k, planes)

    def to_id(k):
        return {"ctx": to_plane(k // 2), "head": y * 2 + k % 2}

    def head_of(k):
        return (to_plane(k // 2) % RING) * 2 + k % 2

    def piece_of(k):
        return (k // 2) * 2 + x

    self_at = (2 - y % 2) * 2 + x

    def z_id(d):
        return {"ctx": lax.rem(z + (RING if d == 0 else 3 * RING), RING * RING)}

    def y_id(o):
        return {"head": lax.rem(y + o, RING) * 2 + x}

    y_step = (1, 3)

    def remote(src, dst, send, recv, where):
        return pltpu.make_async_remote_copy(
            src_ref=src,
            dst_ref=dst,
            send_sem=send,
            recv_sem=recv,
            device_id=where,
            device_id_type=MESH,
        )

    def landed(ref, sem):
        pltpu.make_async_copy(ref, ref, sem).wait()

    raw_lse = pltpu.make_async_copy(lse_in.at[0], lse_raw, raw_sem.at[0])
    raw_delta = pltpu.make_async_copy(delta_in.at[0], delta_raw, raw_sem.at[1])
    raw_lens = pltpu.make_async_copy(lens, lens_held, raw_sem.at[2])
    raw_table = pltpu.make_async_copy(table, table_held, raw_sem.at[3])
    for copy in (raw_lse, raw_delta, raw_lens, raw_table):
        copy.start()

    barrier = pltpu.get_barrier_semaphore()

    def greet(where):
        pl.semaphore_signal(barrier, inc=1, device_id=where, device_id_type=MESH)

    def greet_peer(o, carry):
        greet(from_id(lax.rem(self_at + o, PEERS)))
        return carry

    def greet_up(o, carry):
        greet({**to_id(lax.rem(self_at + o, PEERS)), "section": lax.rem(section + 1, sections)})
        return carry

    lax.fori_loop(1, PEERS, greet_peer, 0)
    for d in range(2):
        greet(z_id(d))
    for o in range(1, RING):
        greet(y_id(o))
    lax.fori_loop(0, PEERS, greet_up, 0)

    part[...] = jnp.zeros_like(part)
    dq[...] = jnp.zeros_like(dq)
    stat_out[...] = jnp.zeros_like(stat_out)
    for copy in (raw_lse, raw_delta, raw_lens, raw_table):
        copy.wait()
    lanes = lax.broadcasted_iota(jnp.int32, (1, BLOCK), 1)
    per_tile = BLOCK // rows
    wide_lse = jnp.concatenate([lse_raw[...]] * per_tile, axis=1) * LOG2E
    wide_delta = jnp.concatenate([delta_raw[...]] * per_tile, axis=1)
    for p in range(PEERS):
        k = lax.rem(z + 2 - y % 2 - p // 2 + planes, RING)
        first_lane = rows * ((k % 2) * 2 + x)
        own_lanes = (lanes >= first_lane) & (lanes < first_lane + rows)
        of_head = slice(p * GROUP, (p + 1) * GROUP)
        stat_out[p, 0:GROUP] = jnp.where(own_lanes, wide_lse[of_head], 0.0)
        stat_out[p, GROUP : 2 * GROUP] = jnp.where(own_lanes, wide_delta[of_head], 0.0)
    pl.semaphore_wait(barrier, 2 * PEERS - 1 + 2 + RING - 1)

    def narrow(h):
        return pl.ds(pl.multiple_of(h * D, D), D)

    def wide(h):
        return pl.ds(pl.multiple_of(h * width, width), width)

    def rows_of(p):
        return pl.ds(pl.multiple_of(p * rows, rows), rows)

    def kv_copies(k):
        return tuple(
            remote(
                src.at[0, :, narrow(head_of(k))],
                kv.at[region_of(k), i, rows_of(piece_of(k))],
                in_send.at[i, k],
                kv_sem,
                to_id(k),
            )
            for i, src in enumerate((k_in, v_in))
        )

    def region_of(k):
        return to_plane(k // 2) // RING

    def q_copies(k):
        return tuple(
            remote(
                src.at[0, :, wide(head_of(k))],
                qg.at[y, piece_of(k), i],
                in_send.at[2 + i, k],
                q_sem.at[piece_of(k)],
                to_id(k),
            )
            for i, src in enumerate((q_in, g_in))
        )

    def stat_copies(k):
        return (
            remote(
                stat_out.at[head_of(k)],
                stat_in.at[piece_of(k)],
                in_send.at[4, k],
                stat_sem,
                to_id(k),
            ),
        )

    def to_peers(copies):
        def one(o, carry):
            for copy in copies(lax.rem(self_at + o, PEERS)):
                copy.start()
            return carry

        lax.fori_loop(1, PEERS, one, 0)

    to_peers(kv_copies)
    for i, src in enumerate((k_in, v_in)):
        pltpu.make_async_copy(src.at[0, :, narrow(mine)], kv.at[region, i, rows_of(self_at)], kv_sem).start()
    to_peers(stat_copies)
    pltpu.make_async_copy(stat_out.at[mine], stat_in.at[self_at], stat_sem).start()
    to_peers(q_copies)
    for i, src in enumerate((q_in, g_in)):
        pltpu.make_async_copy(src.at[0, :, wide(mine)], qg.at[y, self_at, i], q_sem.at[self_at]).start()

    def region_at(o):
        return lax.rem(region + o, RING)

    def tile_of(c):
        return pl.ds(c * BLOCK, BLOCK)

    def ag1(d, i, c):
        held = kv.at[region, i, tile_of(c)]
        return remote(held, held, ag1_send.at[d, i, c], ag1_recv.at[d, i, c], z_id(d))

    def ag1_landed(d, i, c):
        landed(kv.at[region_at(3 if d == 0 else 1), i, tile_of(c)], ag1_recv.at[d, i, c])

    def ag2(d, c):
        held = kv.at[region_at(3 if d == 0 else 1), d, tile_of(c)]
        return remote(held, held, ag2_send.at[d, c], ag2_recv.at[d, c], z_id(d))

    def y_at(o):
        return lax.rem(y + o, RING)

    def yq1(p, d):
        held = qg.at[y, p]
        return remote(held, held, yq1_send.at[d, p], yq1_recv.at[d, p], y_id(y_step[d]))

    def yq1_landed(p, d):
        landed(qg.at[y_at(3 if d == 0 else 1), p], yq1_recv.at[d, p])

    def yq2(p, d):
        held = qg.at[y_at(3 if d == 0 else 1), p]
        return remote(held, held, yq2_send.at[p], yq2_recv.at[p], y_id(y_step[d]))

    def yt(o):
        return remote(stat.at[y], stat.at[y], yt_send.at[o], yt_recv.at[o], y_id(o))

    def pass_own(p):
        landed(qg.at[y, p], q_sem.at[p])
        for d in range(2):
            yq1(p, d).start()

    def nearest(odd, j):
        even_first = (2, 1, 3, 0)[j]
        return even_first + odd * ((1, 0, 2, 3)[j] - even_first)

    pass_own(self_at)
    landed(kv.at[region], kv_sem)
    for i in range(2):
        for c in range(2):
            for d in range(2):
                ag1(d, (i + d) % 2, c).start()
    for j in range(RING):
        u = nearest(y % 2, j)
        if j == 0:
            pass_own(2 * u + 1 - x)
        else:
            pass_own(2 * u)
            pass_own(2 * u + 1)

    landed(stat_in, stat_sem)
    for b in range(2):
        first = b * per_tile
        total = stat_in[first]
        for p in range(1, per_tile):
            total = total + stat_in[first + p]
        stat[y, b] = total
    for o in range(1, RING):
        yt(o).start()


    def lay_out(at):
        for b in range(2):
            for i, stack, turned in ((0, q_stack, q_turned), (1, g_stack, g_turned)):
                tile = qg[at, b * per_tile : (b + 1) * per_tile, i].reshape(BLOCK, width)
                for h in range(GROUP):
                    piece = slice((b * GROUP + h) * BLOCK, (b * GROUP + h + 1) * BLOCK)
                    own = tile[:, h * D : (h + 1) * D]
                    stack[at, piece, :] = own
                    turned[at, :, piece] = own.T

    ends = [lens_held[0, 0]]
    for i in range(1, lens.shape[1]):
        ends.append(ends[-1] + lens_held[0, i])
    run_lanes = lanes % RUN
    run_rows = lax.broadcasted_iota(jnp.int32, (RUN, BLOCK), 0)

    def visit(yq, r, first, count):
        held = pl.ds(first, count)
        key_start = (y % 2) * RUN
        key_places = jnp.concatenate(
            [
                table_held[y // 2, piece_plane(r * RING + plane, y, first // RUN + u)] * BLOCK + key_start + run_rows
                for u in range(count // RUN)
            ],
            axis=0,
        )
        keys, values = kv[r, 0, held], kv[r, 1, held]
        turned_keys = keys.T
        scores = jnp.dot(keys, q_turned[yq], preferred_element_type=jnp.float32)
        grads = jnp.dot(values, g_turned[yq], preferred_element_type=jnp.float32)
        weights, dscores = [], []
        for b in range(2):
            starts_at = [table_held[yq // 2, piece_plane(z, yq, 2 * b + u)] * BLOCK for u in range(2)]
            places = jnp.where(lanes < RUN, starts_at[0], starts_at[1]) + (yq % 2) * RUN + run_lanes
            starts = jnp.zeros_like(places)
            for end in ends:
                starts = jnp.where(places >= end, jnp.maximum(starts, end), starts)
            live = (key_places <= places) & (key_places >= starts)
            totals = stat[yq, b]
            for h in range(GROUP):
                at = slice((b * GROUP + h) * BLOCK, (b * GROUP + h + 1) * BLOCK)
                exponent = scores[:, at] * (scale * LOG2E) - totals[h : h + 1, :]
                weight = jnp.where(live, jnp.exp2(exponent), 0.0)
                dscore = weight * (grads[:, at] - totals[GROUP + h : GROUP + h + 1, :])
                weights.append(weight.astype(jnp.bfloat16))
                dscores.append(dscore.astype(jnp.bfloat16))
        weight16 = jnp.concatenate(weights, axis=1)
        dscore16 = jnp.concatenate(dscores, axis=1)
        part[r, 0, held] += jnp.dot(dscore16, q_stack[yq], preferred_element_type=jnp.float32)
        part[r, 1, held] += jnp.dot(weight16, g_stack[yq], preferred_element_type=jnp.float32)
        dq_all = jnp.dot(turned_keys, dscore16, preferred_element_type=jnp.float32)
        for b in range(2):
            dq[yq, b] += dq_all[:, b * width : (b + 1) * width]

    def z1(d, c):
        return remote(
            zs1.at[d, tile_of(c)], zr1.at[d, tile_of(c)], z1_send.at[d, c], z1_recv.at[d, c], z_id(d)
        )

    def z2(d, i, c):
        return remote(
            zs2.at[d, i, tile_of(c)],
            zr2.at[d, i, tile_of(c)],
            z2_send.at[d, i, c],
            z2_recv.at[d, i, c],
            z_id(d),
        )

    def y1(d):
        return remote(ys1.at[d], yr1.at[d], y1_send.at[d], y1_recv.at[d], y_id(y_step[d]))

    def y2(d, b):
        return remote(ys2.at[d, b], yr2.at[d, b], y2_send.at[d, b], y2_recv.at[d, b], y_id(y_step[d]))

    def visit_live(yq, r, first, count):
        @pl.when((y < 2) | (yq >= 2))
        def _():
            visit(yq, r, first, count)

    def turn(i, carry):
        yq = y_at(pick(i // 3, (0, 1, 3)))

        @pl.when(i == 1)
        def _():
            for j in range(RING):
                for d in range(2):
                    p = 2 * nearest(1 - y % 2, j) + d
                    yq1_landed(p, d)
                    yq2(p, d).start()
                if j in AG_AT:
                    c = AG_AT.index(j)
                    for d in range(2):
                        ag1_landed(d, d, c)
                        ag2(d, c).start()
            for c in range(2):
                for d in range(2):
                    ag1_landed(d, 1 - d, c)

        @pl.when(i == 3)
        def _():
            for p in range(0, PEERS, 2):
                yq1_landed(p, 1)
            landed(stat.at[y_at(1)], yt_recv.at[3])

        @pl.when(i == 6)
        def _():
            for p in range(1, PEERS, 2):
                yq1_landed(p, 0)
            landed(stat.at[y_at(3)], yt_recv.at[1])

        @pl.when(i % 3 == 0)
        def _():
            lay_out(yq)

        visit_live(yq, region_at(pick(i % 3, (0, 1, 3))), 0, 2 * BLOCK)
        return carry

    lax.fori_loop(0, 9, turn, 0)

    def far_turn(i, carry):
        for c in range(2):

            @pl.when(i == RING * c)
            def _():
                for d in range(2):
                    landed(kv.at[region_at(2), d, tile_of(c)], ag2_recv.at[d, c])

        @pl.when(i == 3)
        def _():
            for p in range(PEERS):
                landed(qg.at[y_at(2), p], yq2_recv.at[p])
            landed(stat.at[y_at(2)], yt_recv.at[2])
            lay_out(y_at(2))

        visit_live(
            y_at(pick(i % RING, (0, 1, 3, 2))),
            region_at(2),
            pl.multiple_of(i // RING * BLOCK, BLOCK),
            BLOCK,
        )
        for c in range(2):

            @pl.when(i == RING * c + 3)
            def _():
                for d in range(2):
                    zs1[d, tile_of(c)] = part[region_at(2), d, tile_of(c)].astype(jnp.bfloat16)
                    z1(d, c).start()

        return carry

    lax.fori_loop(0, 2 * RING, far_turn, 0)

    def last_turn(i, carry):
        @pl.when(i == 2)
        def _():
            for d in range(2):
                side = region_at(1 if d == 0 else 3)
                zs2[d, 1 - d] = part[side, 1 - d].astype(jnp.bfloat16)
                for c in range(2):
                    z2(d, 1 - d, c).start()

        visit_live(y_at(2), region_at(pick(i, (1, 3, 0))), 0, 2 * BLOCK)
        return carry

    lax.fori_loop(0, 3, last_turn, 0)

    for d in range(2):
        ys1[d] = dq[y_at(2), d].astype(jnp.bfloat16)
        y1(d).start()
    for d in range(2):
        ys2[d, 1 - d] = dq[y_at(y_step[d]), 1 - d].astype(jnp.bfloat16)
        y2(d, 1 - d).start()
    for d in range(2):
        landed(yr1.at[d], y1_recv.at[d])
        total = dq[y_at(y_step[d]), d] + yr1[d].astype(jnp.float32)
        ys2[d, d] = total.astype(jnp.bfloat16)
        y2(d, d).start()
    for c in range(2):
        for d in range(2):
            landed(zr1.at[d, tile_of(c)], z1_recv.at[d, c])
            side = region_at(1 if d == 0 else 3)
            total = part[side, d, tile_of(c)] + zr1[d, tile_of(c)].astype(jnp.float32)
            zs2[d, d, tile_of(c)] = total.astype(jnp.bfloat16)
            z2(d, d, c).start()

    down = lax.rem(section + sections - 1, sections)

    def out_copy(array, p):
        src, dst, columns = (
            (oq, gq_out, wide(mine)),
            (okv.at[0], gk_out, narrow(mine)),
            (okv.at[1], gv_out, narrow(mine)),
        )[array]
        return remote(
            src.at[rows_of(p)],
            dst.at[0, :, columns],
            out_send.at[array, p],
            out_recv.at[array],
            {**from_id(p), "section": down},
        )

    def hand_over(array):
        def one(o, carry):
            out_copy(array, lax.rem(self_at + o, PEERS)).start()
            return carry

        lax.fori_loop(0, PEERS, one, 0)

    for b in range(2):
        total = dq[y, b]
        for d in range(2):
            landed(yr2.at[d, b], y2_recv.at[d, b])
            total = total + yr2[d, b].astype(jnp.float32)
        total = total * scale
        for h in range(GROUP):
            oq[b * BLOCK : (b + 1) * BLOCK, h * D : (h + 1) * D] = (
                total[:, h * BLOCK : (h + 1) * BLOCK].T.astype(jnp.bfloat16)
            )
    hand_over(0)
    for i in range(2):
        total = part[region, i]
        for d in range(2):
            for c in range(2):
                landed(zr2.at[d, i, tile_of(c)], z2_recv.at[d, i, c])
            total = total + zr2[d, i].astype(jnp.float32)
        okv[i] = (total * scale if i == 0 else total).astype(jnp.bfloat16)
        hand_over(1 + i)

    def end_in(o, carry):
        k = lax.rem(self_at + o, PEERS)
        for copy in kv_copies(k) + q_copies(k) + stat_copies(k):
            copy.wait_send()
        return carry

    lax.fori_loop(1, PEERS, end_in, 0)
    for d in range(2):
        for i in range(2):
            for c in range(2):
                ag1(d, i, c).wait_send()
                z2(d, i, c).wait_send()
            y2(d, i).wait_send()
        for c in range(2):
            ag2(d, c).wait_send()
            z1(d, c).wait_send()
        y1(d).wait_send()
    for o in range(1, RING):
        yt(o).wait_send()
    for p in range(PEERS):
        for d in range(2):
            yq1(p, d).wait_send()
        yq2(p, p % 2).wait_send()

    def end_out(p, carry):
        for array in range(3):
            out_copy(array, p).wait_send()
        return carry

    lax.fori_loop(0, PEERS, end_out, 0)
    for array, out in enumerate((gq_out, gk_out, gv_out)):
        landed(out, out_recv.at[array])


def settle(*refs):
    loads = [pltpu.make_async_copy(refs[i], refs[6 + i], refs[9].at[0, i]) for i in range(3)]
    stores = [pltpu.make_async_copy(refs[6 + i], refs[3 + i], refs[9].at[1, i]) for i in range(3)]
    for copy in loads:
        copy.start()
    for load, store in zip(loads, stores):
        load.wait()
        store.start()
    for copy in stores:
        copy.wait()


def body(q, k, v, g, lse, delta, lens, table):
    rows = q.shape[1]
    tokens = rows * PEERS
    width = GROUP * D
    pieces = tokens * GROUP
    bf16, f32 = jnp.bfloat16, jnp.float32
    any_space = pl.BlockSpec(memory_space=pl.ANY)
    dma = pltpu.SemaphoreType.DMA
    handed = pl.pallas_call(
        kernel,
        out_shape=(
            jax.ShapeDtypeStruct(q.shape, bf16),
            jax.ShapeDtypeStruct(k.shape, bf16),
            jax.ShapeDtypeStruct(v.shape, bf16),
        ),
        in_specs=[any_space] * 8,
        out_specs=(any_space,) * 3,
        scratch_shapes=[
            pltpu.VMEM((RING, PEERS, 2, rows, width), bf16),
            pltpu.VMEM((RING, pieces, D), bf16),
            pltpu.VMEM((RING, pieces, D), bf16),
            pltpu.VMEM((RING, D, pieces), bf16),
            pltpu.VMEM((RING, D, pieces), bf16),
            pltpu.VMEM((RING, 2, tokens, D), bf16),
            pltpu.VMEM((lse.shape[1], rows), f32),
            pltpu.VMEM((lse.shape[1], rows), f32),
            pltpu.VMEM((PEERS, 8, BLOCK), f32),
            pltpu.VMEM((PEERS, 8, BLOCK), f32),
            pltpu.VMEM((RING, 2, 8, BLOCK), f32),
            pltpu.VMEM((RING, 2, D, width), f32),
            pltpu.VMEM((RING, 2, tokens, D), f32),
            pltpu.VMEM((2, tokens, D), bf16),
            pltpu.VMEM((2, tokens, D), bf16),
            pltpu.VMEM((2, 2, tokens, D), bf16),
            pltpu.VMEM((2, 2, tokens, D), bf16),
            pltpu.VMEM((2, D, width), bf16),
            pltpu.VMEM((2, D, width), bf16),
            pltpu.VMEM((2, 2, D, width), bf16),
            pltpu.VMEM((2, 2, D, width), bf16),
            pltpu.VMEM((tokens, width), bf16),
            pltpu.VMEM((2, tokens, D), bf16),
            pltpu.SMEM(lens.shape, jnp.int32),
            pltpu.SMEM(table.shape[::-1], jnp.int32),
            dma((4,)),
            dma,
            dma((PEERS,)),
            dma,
            dma((5, PEERS)),
            dma((2, 2, 2)),
            dma((2, 2, 2)),
            dma((2, 2)),
            dma((2, 2)),
            dma((2, PEERS)),
            dma((2, PEERS)),
            dma((PEERS,)),
            dma((PEERS,)),
            dma((RING,)),
            dma((RING,)),
            dma((2, 2)),
            dma((2, 2)),
            dma((2, 2, 2)),
            dma((2, 2, 2)),
            dma((2,)),
            dma((2,)),
            dma((2, 2)),
            dma((2, 2)),
            dma((3, PEERS)),
            dma((3,)),
        ],
        compiler_params=pltpu.CompilerParams(
            collective_id=0, has_side_effects=True, vmem_limit_bytes=60 * 1024 * 1024
        ),
    )(lens, table.T, q, k, v, g, lse, delta)
    return pl.pallas_call(
        settle,
        out_shape=tuple(jax.ShapeDtypeStruct(out.shape, out.dtype) for out in handed),
        in_specs=[any_space] * 3,
        out_specs=(any_space,) * 3,
        scratch_shapes=[pltpu.VMEM(out.shape, out.dtype) for out in handed] + [dma((2, 3))],
        compiler_params=pltpu.CompilerParams(vmem_limit_bytes=60 * 1024 * 1024),
    )(*handed)


def solution(mesh):
    tokens = P("section", ("ctx", "head"), None)
    totals = P("section", None, ("ctx", "head"))
    return jax.shard_map(
        body,
        mesh=mesh,
        in_specs=(tokens, tokens, tokens, tokens, totals, totals, P("section", None), P()),
        out_specs=(tokens, tokens, tokens),
        check_vma=False,
    )
```

```python
import functools

import jax
import jax.numpy as jnp
from jax import lax
from jax.experimental import pallas as pl
from jax.experimental.pallas import tpu as pltpu
from jax.sharding import PartitionSpec as P

D = 128
BLOCK = 128
GROUP = 3
RING = 4
PEERS = 8
RUN = 64
LOG2E = 1.4426950408889634
AG_AT = (0, 1)
MESH = pl.DeviceIdType.MESH


def pick(i, values):
    return sum(jnp.where(i == k, v, 0) for k, v in enumerate(values) if v)


def kernel(
    lens,
    table,
    q_in,
    k_in,
    v_in,
    g_in,
    lse_in,
    delta_in,
    gq_out,
    gk_out,
    gv_out,
    qg,
    q_stack,
    g_stack,
    q_turned,
    g_turned,
    kv,
    lse_raw,
    delta_raw,
    stat_out,
    stat_in,
    stat,
    dq,
    part,
    zs1,
    zr1,
    zs2,
    zr2,
    ys1,
    yr1,
    ys2,
    yr2,
    oq,
    okv,
    lens_held,
    table_held,
    raw_sem,
    kv_sem,
    q_sem,
    stat_sem,
    in_send,
    ag1_send,
    ag1_recv,
    ag2_send,
    ag2_recv,
    yq1_send,
    yq1_recv,
    yq2_send,
    yq2_recv,
    yt_send,
    yt_recv,
    z1_send,
    z1_recv,
    z2_send,
    z2_recv,
    y1_send,
    y1_recv,
    y2_send,
    y2_recv,
    out_send,
    out_recv,
):
    rows = q_in.shape[1]
    width = GROUP * D
    scale = D ** (-0.5)
    sections = lax.axis_size("section")
    z, place, section = lax.axis_index("ctx"), lax.axis_index("head"), lax.axis_index("section")
    planes = RING * RING
    region, plane = z // RING, z % RING
    y, x = place // 2, place % 2
    mine = plane * 2 + x

    def piece_plane(at, along_y, u):
        return lax.rem(at + planes - 2 + along_y % 2 + u, planes)

    def from_id(p):
        return {"ctx": piece_plane(z, y, p // 2), "head": y * 2 + p % 2}

    def to_plane(k):
        return lax.rem(z + planes + 2 - y % 2 - k, planes)

    def to_id(k):
        return {"ctx": to_plane(k // 2), "head": y * 2 + k % 2}

    def head_of(k):
        return (to_plane(k // 2) % RING) * 2 + k % 2

    def piece_of(k):
        return (k // 2) * 2 + x

    self_at = (2 - y % 2) * 2 + x

    def z_id(d):
        return {"ctx": lax.rem(z + (RING if d == 0 else 3 * RING), RING * RING)}

    def y_id(o):
        return {"head": lax.rem(y + o, RING) * 2 + x}

    y_step = (1, 3)

    def remote(src, dst, send, recv, where):
        return pltpu.make_async_remote_copy(
            src_ref=src,
            dst_ref=dst,
            send_sem=send,
            recv_sem=recv,
            device_id=where,
            device_id_type=MESH,
        )

    def landed(ref, sem):
        pltpu.make_async_copy(ref, ref, sem).wait()

    raw_lse = pltpu.make_async_copy(lse_in.at[0], lse_raw, raw_sem.at[0])
    raw_delta = pltpu.make_async_copy(delta_in.at[0], delta_raw, raw_sem.at[1])
    raw_lens = pltpu.make_async_copy(lens, lens_held, raw_sem.at[2])
    raw_table = pltpu.make_async_copy(table, table_held, raw_sem.at[3])
    for copy in (raw_lse, raw_delta, raw_lens, raw_table):
        copy.start()

    barrier = pltpu.get_barrier_semaphore()

    def greet(where):
        pl.semaphore_signal(barrier, inc=1, device_id=where, device_id_type=MESH)

    def greet_peer(o, carry):
        greet(from_id(lax.rem(self_at + o, PEERS)))
        return carry

    def greet_up(o, carry):
        greet({**to_id(lax.rem(self_at + o, PEERS)), "section": lax.rem(section + 1, sections)})
        return carry

    lax.fori_loop(1, PEERS, greet_peer, 0)
    for d in range(2):
        greet(z_id(d))
    for o in range(1, RING):
        greet(y_id(o))
    lax.fori_loop(0, PEERS, greet_up, 0)

    part[...] = jnp.zeros_like(part)
    dq[...] = jnp.zeros_like(dq)
    stat_out[...] = jnp.zeros_like(stat_out)
    for copy in (raw_lse, raw_delta, raw_lens, raw_table):
        copy.wait()
    lanes = lax.broadcasted_iota(jnp.int32, (1, BLOCK), 1)
    per_tile = BLOCK // rows
    wide_lse = jnp.concatenate([lse_raw[...]] * per_tile, axis=1) * LOG2E
    wide_delta = jnp.concatenate([delta_raw[...]] * per_tile, axis=1)
    for p in range(PEERS):
        k = lax.rem(z + 2 - y % 2 - p // 2 + planes, RING)
        first_lane = rows * ((k % 2) * 2 + x)
        own_lanes = (lanes >= first_lane) & (lanes < first_lane + rows)
        of_head = slice(p * GROUP, (p + 1) * GROUP)
        stat_out[p, 0:GROUP] = jnp.where(own_lanes, wide_lse[of_head], 0.0)
        stat_out[p, GROUP : 2 * GROUP] = jnp.where(own_lanes, wide_delta[of_head], 0.0)
    pl.semaphore_wait(barrier, 2 * PEERS - 1 + 2 + RING - 1)

    def narrow(h):
        return pl.ds(pl.multiple_of(h * D, D), D)

    def wide(h):
        return pl.ds(pl.multiple_of(h * width, width), width)

    def rows_of(p):
        return pl.ds(pl.multiple_of(p * rows, rows), rows)

    def kv_copies(k):
        return tuple(
            remote(
                src.at[0, :, narrow(head_of(k))],
                kv.at[region_of(k), i, rows_of(piece_of(k))],
                in_send.at[i, k],
                kv_sem,
                to_id(k),
            )
            for i, src in enumerate((k_in, v_in))
        )

    def region_of(k):
        return to_plane(k // 2) // RING

    def q_copies(k):
        return tuple(
            remote(
                src.at[0, :, wide(head_of(k))],
                qg.at[y, piece_of(k), i],
                in_send.at[2 + i, k],
                q_sem.at[piece_of(k)],
                to_id(k),
            )
            for i, src in enumerate((q_in, g_in))
        )

    def stat_copies(k):
        return (
            remote(
                stat_out.at[head_of(k)],
                stat_in.at[piece_of(k)],
                in_send.at[4, k],
                stat_sem,
                to_id(k),
            ),
        )

    def to_peers(copies):
        def one(o, carry):
            for copy in copies(lax.rem(self_at + o, PEERS)):
                copy.start()
            return carry

        lax.fori_loop(1, PEERS, one, 0)

    to_peers(kv_copies)
    for i, src in enumerate((k_in, v_in)):
        pltpu.make_async_copy(src.at[0, :, narrow(mine)], kv.at[region, i, rows_of(self_at)], kv_sem).start()
    to_peers(stat_copies)
    pltpu.make_async_copy(stat_out.at[mine], stat_in.at[self_at], stat_sem).start()
    to_peers(q_copies)
    for i, src in enumerate((q_in, g_in)):
        pltpu.make_async_copy(src.at[0, :, wide(mine)], qg.at[y, self_at, i], q_sem.at[self_at]).start()

    def region_at(o):
        return lax.rem(region + o, RING)

    def tile_of(c):
        return pl.ds(c * BLOCK, BLOCK)

    def ag1(d, i, c):
        held = kv.at[region, i, tile_of(c)]
        return remote(held, held, ag1_send.at[d, i, c], ag1_recv.at[d, i, c], z_id(d))

    def ag1_landed(d, i, c):
        landed(kv.at[region_at(3 if d == 0 else 1), i, tile_of(c)], ag1_recv.at[d, i, c])

    def ag2(d, c):
        held = kv.at[region_at(3 if d == 0 else 1), d, tile_of(c)]
        return remote(held, held, ag2_send.at[d, c], ag2_recv.at[d, c], z_id(d))

    def y_at(o):
        return lax.rem(y + o, RING)

    def yq1(p, d):
        held = qg.at[y, p]
        return remote(held, held, yq1_send.at[d, p], yq1_recv.at[d, p], y_id(y_step[d]))

    def yq1_landed(p, d):
        landed(qg.at[y_at(3 if d == 0 else 1), p], yq1_recv.at[d, p])

    def yq2(p, d):
        held = qg.at[y_at(3 if d == 0 else 1), p]
        return remote(held, held, yq2_send.at[p], yq2_recv.at[p], y_id(y_step[d]))

    def yt(o):
        return remote(stat.at[y], stat.at[y], yt_send.at[o], yt_recv.at[o], y_id(o))

    def pass_own(p):
        landed(qg.at[y, p], q_sem.at[p])
        for d in range(2):
            yq1(p, d).start()

    def nearest(odd, j):
        even_first = (2, 1, 3, 0)[j]
        return even_first + odd * ((1, 0, 2, 3)[j] - even_first)

    pass_own(self_at)
    landed(kv.at[region], kv_sem)
    for i in range(2):
        for c in range(2):
            for d in range(2):
                ag1(d, (i + d) % 2, c).start()
    for j in range(RING):
        u = nearest(y % 2, j)
        if j == 0:
            pass_own(2 * u + 1 - x)
        else:
            pass_own(2 * u)
            pass_own(2 * u + 1)

    landed(stat_in, stat_sem)
    for b in range(2):
        first = b * per_tile
        total = stat_in[first]
        for p in range(1, per_tile):
            total = total + stat_in[first + p]
        stat[y, b] = total
    for o in range(1, RING):
        yt(o).start()


    def lay_out(at):
        for b in range(2):
            for i, stack, turned in ((0, q_stack, q_turned), (1, g_stack, g_turned)):
                tile = qg[at, b * per_tile : (b + 1) * per_tile, i].reshape(BLOCK, width)
                for h in range(GROUP):
                    piece = slice((b * GROUP + h) * BLOCK, (b * GROUP + h + 1) * BLOCK)
                    own = tile[:, h * D : (h + 1) * D]
                    stack[at, piece, :] = own
                    turned[at, :, piece] = own.T

    ends = [lens_held[0, 0]]
    for i in range(1, lens.shape[1]):
        ends.append(ends[-1] + lens_held[0, i])
    run_lanes = lanes % RUN
    run_rows = lax.broadcasted_iota(jnp.int32, (RUN, BLOCK), 0)

    def visit(yq, r, first, count):
        held = pl.ds(first, count)
        key_start = (y % 2) * RUN
        key_places = jnp.concatenate(
            [
                table_held[y // 2, piece_plane(r * RING + plane, y, first // RUN + u)] * BLOCK + key_start + run_rows
                for u in range(count // RUN)
            ],
            axis=0,
        )
        keys, values = kv[r, 0, held], kv[r, 1, held]
        turned_keys = keys.T
        scores = jnp.dot(keys, q_turned[yq], preferred_element_type=jnp.float32)
        grads = jnp.dot(values, g_turned[yq], preferred_element_type=jnp.float32)
        weights, dscores = [], []
        for b in range(2):
            starts_at = [table_held[yq // 2, piece_plane(z, yq, 2 * b + u)] * BLOCK for u in range(2)]
            places = jnp.where(lanes < RUN, starts_at[0], starts_at[1]) + (yq % 2) * RUN + run_lanes
            starts = jnp.zeros_like(places)
            for end in ends:
                starts = jnp.where(places >= end, jnp.maximum(starts, end), starts)
            live = (key_places <= places) & (key_places >= starts)
            totals = stat[yq, b]
            for h in range(GROUP):
                at = slice((b * GROUP + h) * BLOCK, (b * GROUP + h + 1) * BLOCK)
                exponent = scores[:, at] * (scale * LOG2E) - totals[h : h + 1, :]
                weight = jnp.where(live, jnp.exp2(exponent), 0.0)
                dscore = weight * (grads[:, at] - totals[GROUP + h : GROUP + h + 1, :])
                weights.append(weight.astype(jnp.bfloat16))
                dscores.append(dscore.astype(jnp.bfloat16))
        weight16 = jnp.concatenate(weights, axis=1)
        dscore16 = jnp.concatenate(dscores, axis=1)
        part[r, 0, held] += jnp.dot(dscore16, q_stack[yq], preferred_element_type=jnp.float32)
        part[r, 1, held] += jnp.dot(weight16, g_stack[yq], preferred_element_type=jnp.float32)
        dq_all = jnp.dot(turned_keys, dscore16, preferred_element_type=jnp.float32)
        for b in range(2):
            dq[yq, b] += dq_all[:, b * width : (b + 1) * width]

    def z1(d, c):
        return remote(
            zs1.at[d, tile_of(c)], zr1.at[d, tile_of(c)], z1_send.at[d, c], z1_recv.at[d, c], z_id(d)
        )

    def z2(d, i, c):
        return remote(
            zs2.at[d, i, tile_of(c)],
            zr2.at[d, i, tile_of(c)],
            z2_send.at[d, i, c],
            z2_recv.at[d, i, c],
            z_id(d),
        )

    def y1(d):
        return remote(ys1.at[d], yr1.at[d], y1_send.at[d], y1_recv.at[d], y_id(y_step[d]))

    def y2(d, b):
        return remote(ys2.at[d, b], yr2.at[d, b], y2_send.at[d, b], y2_recv.at[d, b], y_id(y_step[d]))

    def visit_live(yq, r, first, count):
        @pl.when((y < 2) | (yq >= 2))
        def _():
            visit(yq, r, first, count)

    def turn(i, carry):
        yq = y_at(pick(i % 3, (0, 1, 3)))

        @pl.when(i == 1)
        def _():
            for j in range(RING):
                for d in range(2):
                    p = 2 * nearest(1 - y % 2, j) + d
                    yq1_landed(p, d)
                    yq2(p, d).start()
                if j in AG_AT:
                    c = AG_AT.index(j)
                    for d in range(2):
                        ag1_landed(d, d, c)
                        ag2(d, c).start()
            for p in range(0, PEERS, 2):
                yq1_landed(p, 1)
            landed(stat.at[y_at(1)], yt_recv.at[3])

        @pl.when(i == 2)
        def _():
            for p in range(1, PEERS, 2):
                yq1_landed(p, 0)
            landed(stat.at[y_at(3)], yt_recv.at[1])

        @pl.when(i == 3)
        def _():
            for c in range(2):
                for d in range(2):
                    ag1_landed(d, 1 - d, c)

        @pl.when(i < 3)
        def _():
            lay_out(yq)

        visit_live(yq, region_at(pick(i // 3, (0, 1, 3))), 0, 2 * BLOCK)
        return carry

    lax.fori_loop(0, 9, turn, 0)

    def far_turn(i, carry):
        for c in range(2):

            @pl.when(i == RING * c)
            def _():
                for d in range(2):
                    landed(kv.at[region_at(2), d, tile_of(c)], ag2_recv.at[d, c])

        @pl.when(i == 3)
        def _():
            for p in range(PEERS):
                landed(qg.at[y_at(2), p], yq2_recv.at[p])
            landed(stat.at[y_at(2)], yt_recv.at[2])
            lay_out(y_at(2))

        visit_live(
            y_at(pick(i % RING, (0, 1, 3, 2))),
            region_at(2),
            pl.multiple_of(i // RING * BLOCK, BLOCK),
            BLOCK,
        )
        for c in range(2):

            @pl.when(i == RING * c + 3)
            def _():
                for d in range(2):
                    zs1[d, tile_of(c)] = part[region_at(2), d, tile_of(c)].astype(jnp.bfloat16)
                    z1(d, c).start()

        return carry

    lax.fori_loop(0, 2 * RING, far_turn, 0)

    def last_turn(i, carry):
        @pl.when(i == 2)
        def _():
            for d in range(2):
                side = region_at(1 if d == 0 else 3)
                zs2[d, 1 - d] = part[side, 1 - d].astype(jnp.bfloat16)
                for c in range(2):
                    z2(d, 1 - d, c).start()

        visit_live(y_at(2), region_at(pick(i, (1, 3, 0))), 0, 2 * BLOCK)
        return carry

    lax.fori_loop(0, 3, last_turn, 0)

    for d in range(2):
        ys1[d] = dq[y_at(2), d].astype(jnp.bfloat16)
        y1(d).start()
    for d in range(2):
        ys2[d, 1 - d] = dq[y_at(y_step[d]), 1 - d].astype(jnp.bfloat16)
        y2(d, 1 - d).start()
    for d in range(2):
        landed(yr1.at[d], y1_recv.at[d])
        total = dq[y_at(y_step[d]), d] + yr1[d].astype(jnp.float32)
        ys2[d, d] = total.astype(jnp.bfloat16)
        y2(d, d).start()
    for c in range(2):
        for d in range(2):
            landed(zr1.at[d, tile_of(c)], z1_recv.at[d, c])
            side = region_at(1 if d == 0 else 3)
            total = part[side, d, tile_of(c)] + zr1[d, tile_of(c)].astype(jnp.float32)
            zs2[d, d, tile_of(c)] = total.astype(jnp.bfloat16)
            z2(d, d, c).start()

    down = lax.rem(section + sections - 1, sections)

    def out_copy(array, p):
        src, dst, columns = (
            (oq, gq_out, wide(mine)),
            (okv.at[0], gk_out, narrow(mine)),
            (okv.at[1], gv_out, narrow(mine)),
        )[array]
        return remote(
            src.at[rows_of(p)],
            dst.at[0, :, columns],
            out_send.at[array, p],
            out_recv.at[array],
            {**from_id(p), "section": down},
        )

    def hand_over(array):
        def one(o, carry):
            out_copy(array, lax.rem(self_at + o, PEERS)).start()
            return carry

        lax.fori_loop(0, PEERS, one, 0)

    for b in range(2):
        total = dq[y, b]
        for d in range(2):
            landed(yr2.at[d, b], y2_recv.at[d, b])
            total = total + yr2[d, b].astype(jnp.float32)
        total = total * scale
        for h in range(GROUP):
            oq[b * BLOCK : (b + 1) * BLOCK, h * D : (h + 1) * D] = (
                total[:, h * BLOCK : (h + 1) * BLOCK].T.astype(jnp.bfloat16)
            )
    hand_over(0)
    for i in range(2):
        total = part[region, i]
        for d in range(2):
            for c in range(2):
                landed(zr2.at[d, i, tile_of(c)], z2_recv.at[d, i, c])
            total = total + zr2[d, i].astype(jnp.float32)
        okv[i] = (total * scale if i == 0 else total).astype(jnp.bfloat16)
        hand_over(1 + i)

    def end_in(o, carry):
        k = lax.rem(self_at + o, PEERS)
        for copy in kv_copies(k) + q_copies(k) + stat_copies(k):
            copy.wait_send()
        return carry

    lax.fori_loop(1, PEERS, end_in, 0)
    for d in range(2):
        for i in range(2):
            for c in range(2):
                ag1(d, i, c).wait_send()
                z2(d, i, c).wait_send()
            y2(d, i).wait_send()
        for c in range(2):
            ag2(d, c).wait_send()
            z1(d, c).wait_send()
        y1(d).wait_send()
    for o in range(1, RING):
        yt(o).wait_send()
    for p in range(PEERS):
        for d in range(2):
            yq1(p, d).wait_send()
        yq2(p, p % 2).wait_send()

    def end_out(p, carry):
        for array in range(3):
            out_copy(array, p).wait_send()
        return carry

    lax.fori_loop(0, PEERS, end_out, 0)
    for array, out in enumerate((gq_out, gk_out, gv_out)):
        landed(out, out_recv.at[array])


def settle(*refs):
    loads = [pltpu.make_async_copy(refs[i], refs[6 + i], refs[9].at[0, i]) for i in range(3)]
    stores = [pltpu.make_async_copy(refs[6 + i], refs[3 + i], refs[9].at[1, i]) for i in range(3)]
    for copy in loads:
        copy.start()
    for load, store in zip(loads, stores):
        load.wait()
        store.start()
    for copy in stores:
        copy.wait()


def body(q, k, v, g, lse, delta, lens, table):
    rows = q.shape[1]
    tokens = rows * PEERS
    width = GROUP * D
    pieces = tokens * GROUP
    bf16, f32 = jnp.bfloat16, jnp.float32
    any_space = pl.BlockSpec(memory_space=pl.ANY)
    dma = pltpu.SemaphoreType.DMA
    handed = pl.pallas_call(
        kernel,
        out_shape=(
            jax.ShapeDtypeStruct(q.shape, bf16),
            jax.ShapeDtypeStruct(k.shape, bf16),
            jax.ShapeDtypeStruct(v.shape, bf16),
        ),
        in_specs=[any_space] * 8,
        out_specs=(any_space,) * 3,
        scratch_shapes=[
            pltpu.VMEM((RING, PEERS, 2, rows, width), bf16),
            pltpu.VMEM((RING, pieces, D), bf16),
            pltpu.VMEM((RING, pieces, D), bf16),
            pltpu.VMEM((RING, D, pieces), bf16),
            pltpu.VMEM((RING, D, pieces), bf16),
            pltpu.VMEM((RING, 2, tokens, D), bf16),
            pltpu.VMEM((lse.shape[1], rows), f32),
            pltpu.VMEM((lse.shape[1], rows), f32),
            pltpu.VMEM((PEERS, 8, BLOCK), f32),
            pltpu.VMEM((PEERS, 8, BLOCK), f32),
            pltpu.VMEM((RING, 2, 8, BLOCK), f32),
            pltpu.VMEM((RING, 2, D, width), f32),
            pltpu.VMEM((RING, 2, tokens, D), f32),
            pltpu.VMEM((2, tokens, D), bf16),
            pltpu.VMEM((2, tokens, D), bf16),
            pltpu.VMEM((2, 2, tokens, D), bf16),
            pltpu.VMEM((2, 2, tokens, D), bf16),
            pltpu.VMEM((2, D, width), bf16),
            pltpu.VMEM((2, D, width), bf16),
            pltpu.VMEM((2, 2, D, width), bf16),
            pltpu.VMEM((2, 2, D, width), bf16),
            pltpu.VMEM((tokens, width), bf16),
            pltpu.VMEM((2, tokens, D), bf16),
            pltpu.SMEM(lens.shape, jnp.int32),
            pltpu.SMEM(table.shape[::-1], jnp.int32),
            dma((4,)),
            dma,
            dma((PEERS,)),
            dma,
            dma((5, PEERS)),
            dma((2, 2, 2)),
            dma((2, 2, 2)),
            dma((2, 2)),
            dma((2, 2)),
            dma((2, PEERS)),
            dma((2, PEERS)),
            dma((PEERS,)),
            dma((PEERS,)),
            dma((RING,)),
            dma((RING,)),
            dma((2, 2)),
            dma((2, 2)),
            dma((2, 2, 2)),
            dma((2, 2, 2)),
            dma((2,)),
            dma((2,)),
            dma((2, 2)),
            dma((2, 2)),
            dma((3, PEERS)),
            dma((3,)),
        ],
        compiler_params=pltpu.CompilerParams(
            collective_id=0, has_side_effects=True, vmem_limit_bytes=60 * 1024 * 1024
        ),
    )(lens, table.T, q, k, v, g, lse, delta)
    return pl.pallas_call(
        settle,
        out_shape=tuple(jax.ShapeDtypeStruct(out.shape, out.dtype) for out in handed),
        in_specs=[any_space] * 3,
        out_specs=(any_space,) * 3,
        scratch_shapes=[pltpu.VMEM(out.shape, out.dtype) for out in handed] + [dma((2, 3))],
        compiler_params=pltpu.CompilerParams(vmem_limit_bytes=60 * 1024 * 1024),
    )(*handed)


def solution(mesh):
    tokens = P("section", ("ctx", "head"), None)
    totals = P("section", None, ("ctx", "head"))
    return jax.shard_map(
        body,
        mesh=mesh,
        in_specs=(tokens, tokens, tokens, tokens, totals, totals, P("section", None), P()),
        out_specs=(tokens, tokens, tokens),
        check_vma=False,
    )
```

```python
import functools

import jax
import jax.numpy as jnp
from jax import lax
from jax.experimental import pallas as pl
from jax.experimental.pallas import tpu as pltpu
from jax.sharding import PartitionSpec as P

D = 128
BLOCK = 128
GROUP = 3
RING = 4
PEERS = 8
RUN = 64
LOG2E = 1.4426950408889634
AG_AT = (0, 1)
MESH = pl.DeviceIdType.MESH


def pick(i, values):
    return sum(jnp.where(i == k, v, 0) for k, v in enumerate(values) if v)


def kernel(
    lens,
    table,
    q_in,
    k_in,
    v_in,
    g_in,
    lse_in,
    delta_in,
    gq_out,
    gk_out,
    gv_out,
    qg,
    q_stack,
    g_stack,
    q_turned,
    g_turned,
    kv,
    lse_raw,
    delta_raw,
    stat_out,
    stat_in,
    stat,
    dq,
    part,
    zs1,
    zr1,
    zs2,
    zr2,
    ys1,
    yr1,
    ys2,
    yr2,
    oq,
    okv,
    lens_held,
    table_held,
    raw_sem,
    kv_sem,
    q_sem,
    stat_sem,
    in_send,
    ag1_send,
    ag1_recv,
    ag2_send,
    ag2_recv,
    yq1_send,
    yq1_recv,
    yq2_send,
    yq2_recv,
    yt_send,
    yt_recv,
    z1_send,
    z1_recv,
    z2_send,
    z2_recv,
    y1_send,
    y1_recv,
    y2_send,
    y2_recv,
    out_send,
    out_recv,
):
    rows = q_in.shape[1]
    width = GROUP * D
    scale = D ** (-0.5)
    sections = lax.axis_size("section")
    z, place, section = lax.axis_index("ctx"), lax.axis_index("head"), lax.axis_index("section")
    planes = RING * RING
    region, plane = z // RING, z % RING
    y, x = place // 2, place % 2
    mine = plane * 2 + x

    def piece_plane(at, along_y, u):
        return lax.rem(at + planes - 2 + along_y % 2 + u, planes)

    def from_id(p):
        return {"ctx": piece_plane(z, y, p // 2), "head": y * 2 + p % 2}

    def to_plane(k):
        return lax.rem(z + planes + 2 - y % 2 - k, planes)

    def to_id(k):
        return {"ctx": to_plane(k // 2), "head": y * 2 + k % 2}

    def head_of(k):
        return (to_plane(k // 2) % RING) * 2 + k % 2

    def piece_of(k):
        return (k // 2) * 2 + x

    self_at = (2 - y % 2) * 2 + x

    def z_id(d):
        return {"ctx": lax.rem(z + (RING if d == 0 else 3 * RING), RING * RING)}

    def y_id(o):
        return {"head": lax.rem(y + o, RING) * 2 + x}

    y_step = (1, 3)

    def remote(src, dst, send, recv, where):
        return pltpu.make_async_remote_copy(
            src_ref=src,
            dst_ref=dst,
            send_sem=send,
            recv_sem=recv,
            device_id=where,
            device_id_type=MESH,
        )

    def landed(ref, sem):
        pltpu.make_async_copy(ref, ref, sem).wait()

    raw_lse = pltpu.make_async_copy(lse_in.at[0], lse_raw, raw_sem.at[0])
    raw_delta = pltpu.make_async_copy(delta_in.at[0], delta_raw, raw_sem.at[1])
    raw_lens = pltpu.make_async_copy(lens, lens_held, raw_sem.at[2])
    raw_table = pltpu.make_async_copy(table, table_held, raw_sem.at[3])
    for copy in (raw_lse, raw_delta, raw_lens, raw_table):
        copy.start()

    barrier = pltpu.get_barrier_semaphore()

    def greet(where):
        pl.semaphore_signal(barrier, inc=1, device_id=where, device_id_type=MESH)

    def greet_peer(o, carry):
        greet(from_id(lax.rem(self_at + o, PEERS)))
        return carry

    def greet_up(o, carry):
        greet({**to_id(lax.rem(self_at + o, PEERS)), "section": lax.rem(section + 1, sections)})
        return carry

    lax.fori_loop(1, PEERS, greet_peer, 0)
    for d in range(2):
        greet(z_id(d))
    for o in range(1, RING):
        greet(y_id(o))
    lax.fori_loop(0, PEERS, greet_up, 0)

    part[...] = jnp.zeros_like(part)
    dq[...] = jnp.zeros_like(dq)
    stat_out[...] = jnp.zeros_like(stat_out)
    for copy in (raw_lse, raw_delta, raw_lens, raw_table):
        copy.wait()
    lanes = lax.broadcasted_iota(jnp.int32, (1, BLOCK), 1)
    per_tile = BLOCK // rows
    wide_lse = jnp.concatenate([lse_raw[...]] * per_tile, axis=1) * LOG2E
    wide_delta = jnp.concatenate([delta_raw[...]] * per_tile, axis=1)
    for p in range(PEERS):
        k = lax.rem(z + 2 - y % 2 - p // 2 + planes, RING)
        first_lane = rows * ((k % 2) * 2 + x)
        own_lanes = (lanes >= first_lane) & (lanes < first_lane + rows)
        of_head = slice(p * GROUP, (p + 1) * GROUP)
        stat_out[p, 0:GROUP] = jnp.where(own_lanes, wide_lse[of_head], 0.0)
        stat_out[p, GROUP : 2 * GROUP] = jnp.where(own_lanes, wide_delta[of_head], 0.0)
    pl.semaphore_wait(barrier, 2 * PEERS - 1 + 2 + RING - 1)

    def narrow(h):
        return pl.ds(pl.multiple_of(h * D, D), D)

    def wide(h):
        return pl.ds(pl.multiple_of(h * width, width), width)

    def rows_of(p):
        return pl.ds(pl.multiple_of(p * rows, rows), rows)

    def kv_copies(k):
        return tuple(
            remote(
                src.at[0, :, narrow(head_of(k))],
                kv.at[region_of(k), i, rows_of(piece_of(k))],
                in_send.at[i, k],
                kv_sem,
                to_id(k),
            )
            for i, src in enumerate((k_in, v_in))
        )

    def region_of(k):
        return to_plane(k // 2) // RING

    def q_copies(k):
        return tuple(
            remote(
                src.at[0, :, wide(head_of(k))],
                qg.at[y, piece_of(k), i],
                in_send.at[2 + i, k],
                q_sem.at[piece_of(k)],
                to_id(k),
            )
            for i, src in enumerate((q_in, g_in))
        )

    def stat_copies(k):
        return (
            remote(
                stat_out.at[head_of(k)],
                stat_in.at[piece_of(k)],
                in_send.at[4, k],
                stat_sem,
                to_id(k),
            ),
        )

    def to_peers(copies):
        def one(o, carry):
            for copy in copies(lax.rem(self_at + o, PEERS)):
                copy.start()
            return carry

        lax.fori_loop(1, PEERS, one, 0)

    to_peers(kv_copies)
    for i, src in enumerate((k_in, v_in)):
        pltpu.make_async_copy(src.at[0, :, narrow(mine)], kv.at[region, i, rows_of(self_at)], kv_sem).start()
    to_peers(stat_copies)
    pltpu.make_async_copy(stat_out.at[mine], stat_in.at[self_at], stat_sem).start()
    to_peers(q_copies)
    for i, src in enumerate((q_in, g_in)):
        pltpu.make_async_copy(src.at[0, :, wide(mine)], qg.at[y, self_at, i], q_sem.at[self_at]).start()

    def region_at(o):
        return lax.rem(region + o, RING)

    def tile_of(c):
        return pl.ds(c * BLOCK, BLOCK)

    def ag1(d, i, c):
        held = kv.at[region, i, tile_of(c)]
        return remote(held, held, ag1_send.at[d, i, c], ag1_recv.at[d, i, c], z_id(d))

    def ag1_landed(d, i, c):
        landed(kv.at[region_at(3 if d == 0 else 1), i, tile_of(c)], ag1_recv.at[d, i, c])

    def ag2(d, c):
        held = kv.at[region_at(3 if d == 0 else 1), d, tile_of(c)]
        return remote(held, held, ag2_send.at[d, c], ag2_recv.at[d, c], z_id(d))

    def y_at(o):
        return lax.rem(y + o, RING)

    def yq1(p, d):
        held = qg.at[y, p]
        return remote(held, held, yq1_send.at[d, p], yq1_recv.at[d, p], y_id(y_step[d]))

    def yq1_landed(p, d):
        landed(qg.at[y_at(3 if d == 0 else 1), p], yq1_recv.at[d, p])

    def yq2(p, d):
        held = qg.at[y_at(3 if d == 0 else 1), p]
        return remote(held, held, yq2_send.at[p], yq2_recv.at[p], y_id(y_step[d]))

    def yt(o):
        return remote(stat.at[y], stat.at[y], yt_send.at[o], yt_recv.at[o], y_id(o))

    def pass_own(p):
        landed(qg.at[y, p], q_sem.at[p])
        for d in range(2):
            yq1(p, d).start()

    def nearest(odd, j):
        even_first = (2, 1, 3, 0)[j]
        return even_first + odd * ((1, 0, 2, 3)[j] - even_first)

    pass_own(self_at)
    landed(kv.at[region], kv_sem)
    for i in range(2):
        for c in range(2):
            for d in range(2):
                ag1(d, (i + d) % 2, c).start()
    for j in range(RING):
        u = nearest(y % 2, j)
        if j == 0:
            pass_own(2 * u + 1 - x)
        else:
            pass_own(2 * u)
            pass_own(2 * u + 1)

    landed(stat_in, stat_sem)
    for b in range(2):
        first = b * per_tile
        total = stat_in[first]
        for p in range(1, per_tile):
            total = total + stat_in[first + p]
        stat[y, b] = total
    for o in range(1, RING):
        yt(o).start()


    def lay_out(at):
        for b in range(2):
            for i, stack, turned in ((0, q_stack, q_turned), (1, g_stack, g_turned)):
                tile = qg[at, b * per_tile : (b + 1) * per_tile, i].reshape(BLOCK, width)
                for h in range(GROUP):
                    piece = slice((b * GROUP + h) * BLOCK, (b * GROUP + h + 1) * BLOCK)
                    own = tile[:, h * D : (h + 1) * D]
                    stack[at, piece, :] = own
                    turned[at, :, piece] = own.T

    ends = [lens_held[0, 0]]
    for i in range(1, lens.shape[1]):
        ends.append(ends[-1] + lens_held[0, i])
    run_lanes = lanes % RUN
    run_rows = lax.broadcasted_iota(jnp.int32, (RUN, BLOCK), 0)

    def visit(yq, r, first, count):
        held = pl.ds(first, count)
        key_start = (y % 2) * RUN
        key_places = jnp.concatenate(
            [
                table_held[y // 2, piece_plane(r * RING + plane, y, first // RUN + u)] * BLOCK + key_start + run_rows
                for u in range(count // RUN)
            ],
            axis=0,
        )
        keys, values = kv[r, 0, held], kv[r, 1, held]
        turned_keys = keys.T
        scores = jnp.dot(keys, q_turned[yq], preferred_element_type=jnp.float32)
        grads = jnp.dot(values, g_turned[yq], preferred_element_type=jnp.float32)
        weights, dscores = [], []
        for b in range(2):
            starts_at = [table_held[yq // 2, piece_plane(z, yq, 2 * b + u)] * BLOCK for u in range(2)]
            places = jnp.where(lanes < RUN, starts_at[0], starts_at[1]) + (yq % 2) * RUN + run_lanes
            starts = jnp.zeros_like(places)
            for end in ends:
                starts = jnp.where(places >= end, jnp.maximum(starts, end), starts)
            live = (key_places <= places) & (key_places >= starts)
            totals = stat[yq, b]
            for h in range(GROUP):
                at = slice((b * GROUP + h) * BLOCK, (b * GROUP + h + 1) * BLOCK)
                exponent = scores[:, at] * (scale * LOG2E) - totals[h : h + 1, :]
                weight = jnp.where(live, jnp.exp2(exponent), 0.0)
                dscore = weight * (grads[:, at] - totals[GROUP + h : GROUP + h + 1, :])
                weights.append(weight.astype(jnp.bfloat16))
                dscores.append(dscore.astype(jnp.bfloat16))
        weight16 = jnp.concatenate(weights, axis=1)
        dscore16 = jnp.concatenate(dscores, axis=1)
        part[r, 0, held] += jnp.dot(dscore16, q_stack[yq], preferred_element_type=jnp.float32)
        part[r, 1, held] += jnp.dot(weight16, g_stack[yq], preferred_element_type=jnp.float32)
        dq_all = jnp.dot(turned_keys, dscore16, preferred_element_type=jnp.float32)
        for b in range(2):
            dq[yq, b] += dq_all[:, b * width : (b + 1) * width]

    def z1(d, c):
        return remote(
            zs1.at[d, tile_of(c)], zr1.at[d, tile_of(c)], z1_send.at[d, c], z1_recv.at[d, c], z_id(d)
        )

    def z2(d, i, c):
        return remote(
            zs2.at[d, i, tile_of(c)],
            zr2.at[d, i, tile_of(c)],
            z2_send.at[d, i, c],
            z2_recv.at[d, i, c],
            z_id(d),
        )

    def y1(d):
        return remote(ys1.at[d], yr1.at[d], y1_send.at[d], y1_recv.at[d], y_id(y_step[d]))

    def y2(d, b):
        return remote(ys2.at[d, b], yr2.at[d, b], y2_send.at[d, b], y2_recv.at[d, b], y_id(y_step[d]))

    def visit_live(yq, r, first, count):
        @pl.when((y < 2) | (yq >= 2))
        def _():
            visit(yq, r, first, count)

    def turn(i, carry):
        yq = y_at(pick(i % 3, (0, 1, 3)))

        @pl.when(i == 1)
        def _():
            for j in range(RING):
                for d in range(2):
                    p = 2 * nearest(1 - y % 2, j) + d
                    yq1_landed(p, d)
                    yq2(p, d).start()
                if j in AG_AT:
                    c = AG_AT.index(j)
                    for d in range(2):
                        ag1_landed(d, d, c)
                        ag2(d, c).start()
            for p in range(0, PEERS, 2):
                yq1_landed(p, 1)
            landed(stat.at[y_at(1)], yt_recv.at[3])

        @pl.when(i == 2)
        def _():
            for p in range(1, PEERS, 2):
                yq1_landed(p, 0)
            landed(stat.at[y_at(3)], yt_recv.at[1])

        @pl.when(i == 3)
        def _():
            for c in range(2):
                for d in range(2):
                    ag1_landed(d, 1 - d, c)

        @pl.when(i < 3)
        def _():
            lay_out(yq)

        visit_live(yq, region_at(pick(i // 3, (0, 1, 3))), 0, 2 * BLOCK)
        return carry

    lax.fori_loop(0, 9, turn, 0)

    def far_turn(i, carry):
        for c in range(2):

            @pl.when(i == RING * c)
            def _():
                for d in range(2):
                    landed(kv.at[region_at(2), d, tile_of(c)], ag2_recv.at[d, c])

        @pl.when(i == 3)
        def _():
            for p in range(PEERS):
                landed(qg.at[y_at(2), p], yq2_recv.at[p])
            landed(stat.at[y_at(2)], yt_recv.at[2])
            lay_out(y_at(2))

        visit_live(
            y_at(pick(i % RING, (0, 1, 3, 2))),
            region_at(2),
            pl.multiple_of(i // RING * BLOCK, BLOCK),
            BLOCK,
        )
        for c in range(2):

            @pl.when(i == RING * c + 3)
            def _():
                for d in range(2):
                    zs1[d, tile_of(c)] = part[region_at(2), d, tile_of(c)].astype(jnp.bfloat16)
                    z1(d, c).start()

        return carry

    lax.fori_loop(0, 2 * RING, far_turn, 0)

    def last_turn(i, carry):
        for d in range(2):

            @pl.when(i == 1 + d)
            def _(d=d):
                side = region_at(1 if d == 0 else 3)
                zs2[d, 1 - d] = part[side, 1 - d].astype(jnp.bfloat16)
                for c in range(2):
                    z2(d, 1 - d, c).start()

        visit_live(y_at(2), region_at(pick(i, (1, 3, 0))), 0, 2 * BLOCK)
        return carry

    lax.fori_loop(0, 3, last_turn, 0)

    for d in range(2):
        ys1[d] = dq[y_at(2), d].astype(jnp.bfloat16)
        y1(d).start()
    for d in range(2):
        ys2[d, 1 - d] = dq[y_at(y_step[d]), 1 - d].astype(jnp.bfloat16)
        y2(d, 1 - d).start()
    for d in range(2):
        landed(yr1.at[d], y1_recv.at[d])
        total = dq[y_at(y_step[d]), d] + yr1[d].astype(jnp.float32)
        ys2[d, d] = total.astype(jnp.bfloat16)
        y2(d, d).start()
    for c in range(2):
        for d in range(2):
            landed(zr1.at[d, tile_of(c)], z1_recv.at[d, c])
            side = region_at(1 if d == 0 else 3)
            total = part[side, d, tile_of(c)] + zr1[d, tile_of(c)].astype(jnp.float32)
            zs2[d, d, tile_of(c)] = total.astype(jnp.bfloat16)
            z2(d, d, c).start()

    down = lax.rem(section + sections - 1, sections)

    def out_copy(array, p):
        src, dst, columns = (
            (oq, gq_out, wide(mine)),
            (okv.at[0], gk_out, narrow(mine)),
            (okv.at[1], gv_out, narrow(mine)),
        )[array]
        return remote(
            src.at[rows_of(p)],
            dst.at[0, :, columns],
            out_send.at[array, p],
            out_recv.at[array],
            {**from_id(p), "section": down},
        )

    def hand_over(array):
        def one(o, carry):
            out_copy(array, lax.rem(self_at + o, PEERS)).start()
            return carry

        lax.fori_loop(0, PEERS, one, 0)

    for b in range(2):
        total = dq[y, b]
        for d in range(2):
            landed(yr2.at[d, b], y2_recv.at[d, b])
            total = total + yr2[d, b].astype(jnp.float32)
        total = total * scale
        for h in range(GROUP):
            oq[b * BLOCK : (b + 1) * BLOCK, h * D : (h + 1) * D] = (
                total[:, h * BLOCK : (h + 1) * BLOCK].T.astype(jnp.bfloat16)
            )
    hand_over(0)
    for i in range(2):
        total = part[region, i]
        for d in range(2):
            for c in range(2):
                landed(zr2.at[d, i, tile_of(c)], z2_recv.at[d, i, c])
            total = total + zr2[d, i].astype(jnp.float32)
        okv[i] = (total * scale if i == 0 else total).astype(jnp.bfloat16)
        hand_over(1 + i)

    def end_in(o, carry):
        k = lax.rem(self_at + o, PEERS)
        for copy in kv_copies(k) + q_copies(k) + stat_copies(k):
            copy.wait_send()
        return carry

    lax.fori_loop(1, PEERS, end_in, 0)
    for d in range(2):
        for i in range(2):
            for c in range(2):
                ag1(d, i, c).wait_send()
                z2(d, i, c).wait_send()
            y2(d, i).wait_send()
        for c in range(2):
            ag2(d, c).wait_send()
            z1(d, c).wait_send()
        y1(d).wait_send()
    for o in range(1, RING):
        yt(o).wait_send()
    for p in range(PEERS):
        for d in range(2):
            yq1(p, d).wait_send()
        yq2(p, p % 2).wait_send()

    def end_out(p, carry):
        for array in range(3):
            out_copy(array, p).wait_send()
        return carry

    lax.fori_loop(0, PEERS, end_out, 0)
    for array, out in enumerate((gq_out, gk_out, gv_out)):
        landed(out, out_recv.at[array])


def settle(*refs):
    loads = [pltpu.make_async_copy(refs[i], refs[6 + i], refs[9].at[0, i]) for i in range(3)]
    stores = [pltpu.make_async_copy(refs[6 + i], refs[3 + i], refs[9].at[1, i]) for i in range(3)]
    for copy in loads:
        copy.start()
    for load, store in zip(loads, stores):
        load.wait()
        store.start()
    for copy in stores:
        copy.wait()


def body(q, k, v, g, lse, delta, lens, table):
    rows = q.shape[1]
    tokens = rows * PEERS
    width = GROUP * D
    pieces = tokens * GROUP
    bf16, f32 = jnp.bfloat16, jnp.float32
    any_space = pl.BlockSpec(memory_space=pl.ANY)
    dma = pltpu.SemaphoreType.DMA
    handed = pl.pallas_call(
        kernel,
        out_shape=(
            jax.ShapeDtypeStruct(q.shape, bf16),
            jax.ShapeDtypeStruct(k.shape, bf16),
            jax.ShapeDtypeStruct(v.shape, bf16),
        ),
        in_specs=[any_space] * 8,
        out_specs=(any_space,) * 3,
        scratch_shapes=[
            pltpu.VMEM((RING, PEERS, 2, rows, width), bf16),
            pltpu.VMEM((RING, pieces, D), bf16),
            pltpu.VMEM((RING, pieces, D), bf16),
            pltpu.VMEM((RING, D, pieces), bf16),
            pltpu.VMEM((RING, D, pieces), bf16),
            pltpu.VMEM((RING, 2, tokens, D), bf16),
            pltpu.VMEM((lse.shape[1], rows), f32),
            pltpu.VMEM((lse.shape[1], rows), f32),
            pltpu.VMEM((PEERS, 8, BLOCK), f32),
            pltpu.VMEM((PEERS, 8, BLOCK), f32),
            pltpu.VMEM((RING, 2, 8, BLOCK), f32),
            pltpu.VMEM((RING, 2, D, width), f32),
            pltpu.VMEM((RING, 2, tokens, D), f32),
            pltpu.VMEM((2, tokens, D), bf16),
            pltpu.VMEM((2, tokens, D), bf16),
            pltpu.VMEM((2, 2, tokens, D), bf16),
            pltpu.VMEM((2, 2, tokens, D), bf16),
            pltpu.VMEM((2, D, width), bf16),
            pltpu.VMEM((2, D, width), bf16),
            pltpu.VMEM((2, 2, D, width), bf16),
            pltpu.VMEM((2, 2, D, width), bf16),
            pltpu.VMEM((tokens, width), bf16),
            pltpu.VMEM((2, tokens, D), bf16),
            pltpu.SMEM(lens.shape, jnp.int32),
            pltpu.SMEM(table.shape[::-1], jnp.int32),
            dma((4,)),
            dma,
            dma((PEERS,)),
            dma,
            dma((5, PEERS)),
            dma((2, 2, 2)),
            dma((2, 2, 2)),
            dma((2, 2)),
            dma((2, 2)),
            dma((2, PEERS)),
            dma((2, PEERS)),
            dma((PEERS,)),
            dma((PEERS,)),
            dma((RING,)),
            dma((RING,)),
            dma((2, 2)),
            dma((2, 2)),
            dma((2, 2, 2)),
            dma((2, 2, 2)),
            dma((2,)),
            dma((2,)),
            dma((2, 2)),
            dma((2, 2)),
            dma((3, PEERS)),
            dma((3,)),
        ],
        compiler_params=pltpu.CompilerParams(
            collective_id=0, has_side_effects=True, vmem_limit_bytes=60 * 1024 * 1024
        ),
    )(lens, table.T, q, k, v, g, lse, delta)
    return pl.pallas_call(
        settle,
        out_shape=tuple(jax.ShapeDtypeStruct(out.shape, out.dtype) for out in handed),
        in_specs=[any_space] * 3,
        out_specs=(any_space,) * 3,
        scratch_shapes=[pltpu.VMEM(out.shape, out.dtype) for out in handed] + [dma((2, 3))],
        compiler_params=pltpu.CompilerParams(vmem_limit_bytes=60 * 1024 * 1024),
    )(*handed)


def solution(mesh):
    tokens = P("section", ("ctx", "head"), None)
    totals = P("section", None, ("ctx", "head"))
    return jax.shard_map(
        body,
        mesh=mesh,
        in_specs=(tokens, tokens, tokens, tokens, totals, totals, P("section", None), P()),
        out_specs=(tokens, tokens, tokens),
        check_vma=False,
    )
```
